128 devices in a mesh: grp: 4 (over y), dom: 32 (over z, x, core).
Axes of the slice: x: 4, y: 4, z: 4, core: 2. Of those that a mesh axis runs over, the one named last changes fastest.
Arguments:
- right_side: float32 [16, 2048, 16, 128], P(None, ('grp', 'dom')), may hold values from -12 to 12
- diagonal: float32 [2048, 16, 128], P(('grp', 'dom')), may hold values from 1 to 4
- counts: int32 [128], P(('grp', 'dom')), may hold values from 8 to 16, as said below
Outputs:
- solution_field: float32 [16, 2048, 16, 128], P(None, ('grp', 'dom'))
- residual: float32 [16, 2048, 16, 128], P(None, ('grp', 'dom'))
The draws below stay inside these ranges and needn't reach their ends.
Inputs may be any that keep to these rules, and one draw needn't show every extreme that they name: counts[i] live planes of partition i occupy its first plane slots; some partition has all 16 slots live.
All inputs are finite; a program needn't handle non-finite values.
Results may differ from the reference program's by a relative error of at most 0.00035.
Values sent between devices are 32-bit elements; how exact they have to be, the bound alone decides.
No kernel may reach another device: no remote copies, remote signals or barrier semaphores. Data moves between devices by JAX's collectives and lax.ppermute only.
A program may use at most 128 MiB of HBM per device.

```python
import math
import jax
import jax.numpy as jnp
from jax import lax

NRHS = 16
SSTEP = 4
OUTER = 2
CX = 16
NY = 16
NZ = 128
PARTITIONS = 128
PLANES = 2048


def draw_right_side(key, part):
    key = jax.random.fold_in(key, 11)
    shape = (NRHS, PLANES, NY, NZ)
    plane = jnp.arange(PLANES, dtype=jnp.float32)
    rising = (1.0 + 2.0 * plane / max(PLANES - 1, 1))[None, :, None, None]
    values = jnp.clip(jax.random.normal(key, shape, jnp.float32), -4.0, 4.0) * rising
    return values


def draw_counts(key, part):
    key = jax.random.fold_in(key, 5)
    first, second = jax.random.split(key)
    drawn = jax.random.randint(first, (PARTITIONS,), CX // 2, CX + 1)
    chosen = jax.random.randint(second, (), 0, PARTITIONS)
    return jnp.where(jnp.arange(PARTITIONS) == chosen, CX, drawn).astype(jnp.int32)


def shard_levels(key, extent, pieces, low, high):
    gain = 1.0
    for dim, blocks in pieces:
        heights = jax.random.uniform(jax.random.fold_in(jax.random.fold_in(key, 6), dim), (blocks,), jnp.float32, low / len(pieces), high / len(pieces))
        gain = gain * jnp.repeat(jnp.exp(heights), extent[dim] // blocks).reshape((-1,) + (1,) * (len(extent) - 1 - dim))
    return gain


def setup_inputs(seed: int = 0) -> dict:
    keys = jax.random.split(jax.random.key(seed), 4)
    return {
        "right_side": draw_right_side(jax.random.fold_in(keys[3], 71), 0),
        "diagonal": jnp.clip(jnp.exp(math.log(4.0) - 1.3862944 * jax.random.uniform(keys[1], (PLANES, NY, NZ), jnp.float32) ** shard_levels(keys[1], (PLANES, NY, NZ), ((0, 128),), -0.2, 0.2)), 1.0, 4.0),
        "counts": draw_counts(jax.random.fold_in(keys[3], 71), 0),
    }


SHIFT = 8.5
SCALE = 7.5

def apply_op(centre, below, above, diag):
    beside = above + below
    padded = jnp.pad(centre, ((0, 0), (0, 0), (1, 1), (0, 0)))
    beside = beside + padded[:, :, 2:] + padded[:, :, :-2]
    padded = jnp.pad(centre, ((0, 0), (0, 0), (0, 0), (1, 1)))
    beside = beside + padded[..., 2:] + padded[..., :-2]
    return (6.0 + diag) * centre - beside

def change_matrix():
    small = SHIFT * jnp.eye(SSTEP + 1, SSTEP, dtype=jnp.float32) + SCALE * jnp.eye(SSTEP + 1, SSTEP, k=-1, dtype=jnp.float32)
    return jnp.kron(small, jnp.eye(NRHS, dtype=jnp.float32))

def galerkin(gram):
    change = change_matrix()
    leading = gram[:SSTEP * NRHS]
    system = jnp.dot(leading, change, precision=lax.Precision.HIGHEST)
    system = 0.5 * (system + system.T)
    factor = jnp.linalg.cholesky(system)
    coef = jax.scipy.linalg.cho_solve((factor, True), leading[:, :NRHS])
    return (coef, jnp.dot(change, coef, precision=lax.Precision.HIGHEST))

def reference(right_side, diagonal, counts):
    plane = jnp.arange(PLANES, dtype=jnp.int32)
    owner = plane // CX
    local = plane % CX
    count_here = counts[owner]
    live = local < count_here
    owner_low = jnp.maximum(owner - 1, 0)
    owner_high = jnp.minimum(owner + 1, PARTITIONS - 1)
    prev_index = jnp.where(local > 0, plane - 1, owner_low * CX + counts[owner_low] - 1).astype(jnp.int32)
    next_index = jnp.where(local < count_here - 1, plane + 1, owner_high * CX).astype(jnp.int32)
    has_prev = ((local > 0) | (owner > 0))[None, :, None, None]
    has_next = ((local < count_here - 1) | (owner < PARTITIONS - 1))[None, :, None, None]
    live_mask = live[None, :, None, None]

    def operate(field):
        below = jnp.where(has_prev, field[:, prev_index], 0.0)
        above = jnp.where(has_next, field[:, next_index], 0.0)
        return jnp.where(live_mask, apply_op(field, below, above, diagonal), 0.0)
    residual = jnp.where(live_mask, right_side, 0.0)
    solution_field = jnp.zeros_like(right_side)
    for outer in range(OUTER):
        basis = [residual]
        for power in range(SSTEP):
            current = basis[-1]
            image = operate(current)
            basis.append(jnp.where(live_mask, (image - SHIFT * current) / SCALE, 0.0))
        panel = jnp.stack(basis).reshape((SSTEP + 1) * NRHS, -1)
        gram = jnp.dot(panel, panel.T, precision=lax.Precision.HIGHEST)
        coef, step = galerkin(gram)
        solution_field = solution_field + jnp.dot(coef.T, panel[:SSTEP * NRHS], precision=lax.Precision.HIGHEST).reshape(right_side.shape)
        residual = residual - jnp.dot(step.T, panel, precision=lax.Precision.HIGHEST).reshape(right_side.shape)
    return (solution_field, residual)
```

```python
import functools

import jax
import jax.numpy as jnp
from jax import lax
from jax.experimental import pallas as pl
from jax.experimental.pallas import tpu as pltpu
from jax.sharding import PartitionSpec as P

NRHS = 16
SSTEP = 4
SHIFT = 8.5
SCALE = 7.5
CX = 16
NY = 16
NZ = 128
GHOST = 8
KB = SSTEP + 1
PIECE = KB * NRHS
AXES = ("grp", "dom")
F32 = jnp.float32
BF16 = jnp.bfloat16


def pieces(value):
    hi = value.astype(BF16)
    rest = value - hi.astype(F32)
    mid = rest.astype(BF16)
    lo = (rest - mid.astype(F32)).astype(BF16)
    return hi, mid, lo


def store_pieces(panel, plane, y, power, value):
    for i, part in enumerate(pieces(value)):
        panel[plane, y, pl.ds(i * PIECE + power * NRHS, NRHS), :] = part


def plane_step(src, dst, coef, weight, plane, panel, panel_plane, power):
    lane = lax.broadcasted_iota(jnp.int32, (NRHS, NZ), 1)
    first = lane == 0
    last = lane == NZ - 1
    zero = jnp.zeros((NRHS, NZ), F32)
    before = zero
    centre = src[plane, 0]
    for y in range(NY):
        after = src[plane, y + 1] if y + 1 < NY else zero
        beside = src[plane - 1, y] + src[plane + 1, y] + (before + after)
        beside = beside + jnp.where(first, 0.0, pltpu.roll(centre, 1, 1))
        beside = beside + jnp.where(last, 0.0, pltpu.roll(centre, NZ - 1, 1))
        value = coef[plane, pl.ds(y, 1), :] * centre - weight * beside
        if dst is not None:
            dst[plane, y] = value
        if panel is not None:
            store_pieces(panel, panel_plane, y, power, value)
        before, centre = centre, after


def moments(panel, start, stop):
    def body(plane, acc):
        for y in range(0, NY, 2):
            def rows(at, size):
                return jnp.concatenate(
                    [panel[plane, y, pl.ds(at, size), :], panel[plane, y + 1, pl.ds(at, size), :]], 1
                )

            left = jnp.concatenate(
                [rows(0, NRHS), rows(PIECE, NRHS), rows(SSTEP * NRHS, NRHS), rows(PIECE + SSTEP * NRHS, NRHS)], 0
            )
            right = rows(0, 2 * PIECE)
            acc = acc + lax.dot_general(
                left, right, (((1,), (1,)), ((), ())), preferred_element_type=F32
            )
        return acc

    acc = lax.fori_loop(start, stop, body, jnp.zeros((4 * NRHS, 2 * PIECE), F32))
    low = acc[:NRHS] + acc[NRHS : 2 * NRHS]
    high = acc[2 * NRHS : 3 * NRHS] + acc[3 * NRHS :]
    low = low[:, :PIECE] + low[:, PIECE:]
    high = high[:, :PIECE] + high[:, PIECE:]
    return jnp.concatenate([low, high[:, NRHS : 4 * NRHS]], 1)


def solve(mom):
    size = SSTEP * NRHS
    shifted = jnp.concatenate([mom[:, NRHS:], mom[:, :NRHS]], 1)
    band = SHIFT * mom + SCALE * shifted
    blocks = [band[:, i * NRHS : i * NRHS + size] for i in range(SSTEP)]
    right = mom[:, :size]
    work = jnp.concatenate(blocks + [right], 0)
    lane = lax.broadcasted_iota(jnp.int32, (1, size), 1)
    scale = jnp.zeros((1, size), F32)
    for j in range(size):
        base = j // 8 * 8
        tail = work[base:]
        row = tail[j - base : j - base + 1]
        inv = 1.0 / row[:, j : j + 1]
        scale = jnp.where(lane == j, inv, scale)
        row = jnp.where(lane == j, 0.0, row * inv)
        tail = tail - tail[:, j : j + 1] * row
        work = tail if base == 0 else jnp.concatenate([work[:base], tail], 0)
    return work[size:] * scale


def coef_rows(coef_t):
    size = SSTEP * NRHS
    pad = jnp.zeros((NRHS, NRHS), F32)
    eye = (
        lax.broadcasted_iota(jnp.int32, (NRHS, PIECE), 0)
        == lax.broadcasted_iota(jnp.int32, (NRHS, PIECE), 1)
    ).astype(F32)
    same = jnp.concatenate([coef_t, pad], 1)
    up = jnp.concatenate([pad, coef_t], 1)
    left = eye - (SHIFT * same + SCALE * up)
    l_hi, l_mid, l_lo = pieces(left)
    c_hi, c_mid, _ = pieces(same)
    none = jnp.zeros((NRHS, PIECE), BF16)
    rows = [
        [l_hi, l_hi, l_hi],
        [l_mid, l_mid, none],
        [l_lo, none, none],
        [c_hi, c_hi, none],
        [c_mid, none, none],
    ]
    return jnp.concatenate([jnp.concatenate(r, 1) for r in rows], 0)


def combine(coefs, panel, plane, y):
    block = jnp.concatenate([panel[plane, y], panel[plane, y + 1]], 1)
    out = jnp.dot(coefs, block, preferred_element_type=F32)
    left = out[:NRHS] + out[NRHS : 2 * NRHS] + out[2 * NRHS : 3 * NRHS]
    step = out[3 * NRHS : 4 * NRHS] + out[4 * NRHS :]
    return left, step


def first_kernel(info, right, lower, upper, diag, panel, ghosts, coef, mom, field_a, field_b):
    count = info[0]
    has_lower = info[1]
    has_upper = info[2]
    rows = NY * CX
    ghost_rows = GHOST * NY
    total = CX + 2 * GHOST

    def weight_of(plane):
        inside = (
            ((plane >= GHOST) | (has_lower > 0))
            & ((plane < GHOST + count) | (has_upper > 0))
            & (plane < 2 * GHOST + count)
        )
        return jnp.where(inside, 1.0 / SCALE, 0.0).astype(F32)

    def load_own(p, carry):
        live = (p < count).astype(F32)
        for y in range(NY):
            value = right[pl.Slice(p * NY + y, NRHS, rows), :]
            field_a[GHOST + p, y] = value * live
        coef[GHOST + p] = (diag[p] + (6.0 - SHIFT)) * (1.0 / SCALE)
        return carry

    def load_ghost(p, carry):
        for src, at in ((lower, p), (upper, GHOST + count + p)):
            for y in range(NY):
                field_a[at, y] = src[pl.Slice(p * NY + y, NRHS, ghost_rows), :]
            d = src[pl.ds(NRHS * ghost_rows + p * NY, NY), :]
            coef[at] = (d + (6.0 - SHIFT)) * (1.0 / SCALE)
        return carry

    for p in range(GHOST):
        coef[GHOST + CX + p] = jnp.zeros((NY, NZ), F32)
        field_a[GHOST + CX + p] = jnp.zeros((NY, NRHS, NZ), F32)
    lax.fori_loop(0, CX, load_own, 0)
    lax.fori_loop(0, GHOST, load_ghost, 0)

    parts = (
        (SSTEP, GHOST, ghosts, SSTEP),
        (GHOST, GHOST + CX, panel, GHOST),
        (GHOST + CX, total - SSTEP, ghosts, GHOST + CX - SSTEP),
    )
    for start, stop, store, base in parts:

        def split_body(p, carry, store=store, base=base):
            for y in range(NY):
                store_pieces(store, p - base, y, 0, field_a[p, y])
            return carry

        lax.fori_loop(start, stop, split_body, 0)
    fields = (field_a, field_b)
    for power in range(1, SSTEP + 1):
        src, dst = fields[(power - 1) % 2], fields[power % 2]

        def bare(p, carry, src=src, dst=dst, power=power):
            plane_step(src, dst, coef, weight_of(p), p, None, p, power)
            return carry

        if power < SSTEP:
            lax.fori_loop(power, SSTEP, bare, 0)
            lax.fori_loop(total - SSTEP, total - power, bare, 0)
        for start, stop, store, base in parts:

            def full(p, carry, src=src, dst=dst, power=power, store=store, base=base):
                plane_step(src, dst, coef, weight_of(p), p, store, p - base, power)
                return carry

            lax.fori_loop(start, stop, full, 0)
    mom[...] = moments(panel, 0, count)


def middle_kernel(info, mom_in, coef, panel_in, ghosts, panel, mom, iterate, field_a, field_b):
    count = info[0]
    has_lower = info[1]
    has_upper = info[2]
    total = CX + 2 * SSTEP

    def weight_of(plane):
        inside = (
            ((plane >= SSTEP) | (has_lower > 0))
            & ((plane < SSTEP + count) | (has_upper > 0))
            & (plane < 2 * SSTEP + count)
        )
        return jnp.where(inside, 1.0 / SCALE, 0.0).astype(F32)

    coefs = coef_rows(solve(mom_in[...]))

    def update(p, own, store, base, carry):
        for y in range(0, NY, 2):
            left, step = combine(coefs, store, p - base, y)
            for k in range(2):
                value = left[:, k * NZ : (k + 1) * NZ]
                field_a[p, y + k] = value
                if own:
                    store_pieces(panel, p - SSTEP, y + k, 0, value)
                    iterate[p - SSTEP, y + k] = step[:, k * NZ : (k + 1) * NZ]
        return carry

    lax.fori_loop(0, SSTEP, lambda p, c: update(p, False, ghosts, 0, c), 0)
    lax.fori_loop(SSTEP, SSTEP + CX, lambda p, c: update(p, True, panel_in, SSTEP, c), 0)
    lax.fori_loop(SSTEP + CX, total, lambda p, c: update(p, False, ghosts, CX, c), 0)
    shifted = coef.at[pl.ds(SSTEP, total)]
    fields = (field_a, field_b)
    for power in range(1, SSTEP + 1):
        src, dst = fields[(power - 1) % 2], fields[power % 2]
        if power == SSTEP:
            dst = None

        def bare(p, carry, src=src, dst=dst, power=power):
            plane_step(src, dst, shifted, weight_of(p), p, None, p, power)
            return carry

        def full(p, carry, src=src, dst=dst, power=power):
            plane_step(src, dst, shifted, weight_of(p), p, panel, p - SSTEP, power)
            return carry

        if power < SSTEP:
            lax.fori_loop(power, SSTEP, bare, 0)
            lax.fori_loop(total - SSTEP, total - power, bare, 0)
        lax.fori_loop(SSTEP, total - SSTEP, full, 0)
    mom[...] = moments(panel, 0, count)


def last_kernel(info, mom_in, panel, iterate, solution_field, residual):
    count = info[0]
    rows = NY * CX
    coefs = coef_rows(solve(mom_in[...]))

    def live(p, carry):
        for y in range(0, NY, 2):
            left, step = combine(coefs, panel, p, y)
            for k in range(2):
                at = pl.Slice(p * NY + y + k, NRHS, rows)
                residual[at, :] = left[:, k * NZ : (k + 1) * NZ]
                solution_field[at, :] = iterate[p, y + k] + step[:, k * NZ : (k + 1) * NZ]
        return carry

    def dead(p, carry):
        for y in range(NY):
            at = pl.Slice(p * NY + y, NRHS, rows)
            residual[at, :] = jnp.zeros((NRHS, NZ), F32)
            solution_field[at, :] = jnp.zeros((NRHS, NZ), F32)
        return carry

    lax.fori_loop(0, count, live, 0)
    lax.fori_loop(count, CX, dead, 0)


SMEM_SPEC = pl.BlockSpec(memory_space=pltpu.SMEM)
VMEM_SPEC = pl.BlockSpec(memory_space=pltpu.VMEM)


def call(body, limit, operands, outs, scratch, kept_operands=(), aliases={}):
    operands = [
        pltpu.with_memory_space_constraint(x, pltpu.VMEM) if i in kept_operands else x
        for i, x in enumerate(operands)
    ]
    return pl.pallas_call(
        body,
        out_shape=[pltpu.VMEM(s, d) if kept else jax.ShapeDtypeStruct(s, d) for s, d, kept in outs],
        in_specs=[SMEM_SPEC] + [VMEM_SPEC] * (len(operands) - 1),
        out_specs=[VMEM_SPEC] * len(outs),
        scratch_shapes=scratch,
        input_output_aliases=aliases,
        compiler_params=pltpu.CompilerParams(vmem_limit_bytes=limit * 1024 * 1024),
    )(*operands)


def reduce_all(value, size, last):
    rounds = []
    if size == 128:
        rounds = [(1, 2), (2, 4), (8, 4), (32, 4)]
    else:
        stride = 1
        while stride < size:
            rounds.append((stride, 2))
            stride *= 2
    for stride, width in rounds:
        total = value
        for turn in range(1, width):
            route = []
            for i in range(size):
                place = i // stride % width
                route.append((i, i + ((place + turn) % width - place) * stride))
            total = total + lax.ppermute(value, AXES, route)
        value = total
    return value


def local(right_side, diagonal, counts):
    count = counts[0]
    size = lax.axis_size(AXES)
    me = lax.axis_index(AXES)
    info = jnp.stack([count, me, size - 1 - me]).astype(jnp.int32)
    both = jnp.concatenate([right_side, diagonal[None]], 0)
    tops = lax.dynamic_slice_in_dim(both, count - GHOST, GHOST, 1)
    firsts = both[:, :GHOST]
    lower = lax.ppermute(tops, AXES, [(i, i + 1) for i in range(size - 1)])
    upper = lax.ppermute(firsts, AXES, [(i + 1, i) for i in range(size - 1)])
    ghost_shape = ((NRHS + 1) * GHOST * NY, NZ)
    field = (NY, NRHS, NZ)
    total = CX + 2 * GHOST
    middle = CX + 2 * SSTEP
    panel1, ghosts, coef, mom = call(
        first_kernel,
        16,
        (
            info,
            right_side.reshape(NRHS * CX * NY, NZ),
            lower.reshape(ghost_shape),
            upper.reshape(ghost_shape),
            diagonal,
        ),
        [
            ((CX, NY, 3 * PIECE, NZ), BF16, True),
            ((2 * SSTEP, NY, 3 * PIECE, NZ), BF16, True),
            ((total, NY, NZ), F32, True),
            ((NRHS, NZ), F32, False),
        ],
        [pltpu.VMEM((total,) + field, F32), pltpu.VMEM((total,) + field, F32)],
    )
    mom = reduce_all(mom, size, False)
    panel2, mom, iterate = call(
        middle_kernel,
        8,
        (info, mom, coef, panel1, ghosts),
        [
            ((CX, NY, 3 * PIECE, NZ), BF16, True),
            ((NRHS, NZ), F32, False),
            ((CX,) + field, F32, True),
        ],
        [pltpu.VMEM((middle,) + field, F32), pltpu.VMEM((middle,) + field, F32)],
        (2, 3, 4),
    )
    mom = reduce_all(mom, size, True)
    out = (NRHS * CX * NY, NZ)
    solution_field, residual = call(
        last_kernel,
        8,
        (info, mom, panel2, iterate),
        [(out, F32, False), (out, F32, False)],
        [],
        (2, 3),
    )
    return (solution_field.reshape(right_side.shape), residual.reshape(right_side.shape))


def solution(mesh):
    in_specs = (
        P(None, AXES, None, None),
        P(AXES, None, None),
        P(AXES),
    )
    out_specs = (P(None, AXES, None, None), P(None, AXES, None, None))
    return jax.shard_map(local, mesh=mesh, in_specs=in_specs, out_specs=out_specs, check_vma=False)
```

```python
import jax
import jax.numpy as jnp
from jax import lax
from jax.experimental import pallas as pl
from jax.experimental.pallas import tpu as pltpu
from jax.sharding import PartitionSpec as P

NRHS = 16
SSTEP = 4
SHIFT = 8.5
SCALE = 7.5
CX = 16
NY = 16
NZ = 128
KB = SSTEP + 1
PIECE = KB * NRHS
MID = CX - 2 * SSTEP
MIDDLE = CX + 2 * SSTEP
AXES = ("grp", "dom")
F32 = jnp.float32
BF16 = jnp.bfloat16
FIELD = (NY, NRHS, NZ)
PANEL = (NY, 3 * PIECE, NZ)


def over(start, stop, body, group=4):
    whole = (stop - start) // group

    def step(i, carry):
        for k in range(group):
            body(start + i * group + k)
        return carry

    if whole:
        lax.fori_loop(0, whole, step, 0)
    for plane in range(start + whole * group, stop):
        body(plane)


def pieces(value):
    hi = value.astype(BF16)
    rest = value - hi.astype(F32)
    mid = rest.astype(BF16)
    lo = (rest - mid.astype(F32)).astype(BF16)
    return hi, mid, lo


def store_pieces(panel, plane, y, power, value):
    for i, part in enumerate(pieces(value)):
        panel[plane, y, pl.ds(i * PIECE + power * NRHS, NRHS), :] = part


def split_plane(panel, at, power, field, plane):
    for y in range(NY):
        store_pieces(panel, at, y, power, field[plane, y])


def coef_of(diag):
    return (diag + (6.0 - SHIFT)) * (1.0 / SCALE)


def plane_step(below, centre_at, above, coef, weight, emit):
    lane = lax.broadcasted_iota(jnp.int32, (NRHS, NZ), 1)
    first = lane == 0
    last = lane == NZ - 1
    zero = jnp.zeros((NRHS, NZ), F32)
    src, plane = centre_at
    before = zero
    centre = src[plane, 0]
    for y in range(NY):
        after = src[plane, y + 1] if y + 1 < NY else zero
        beside = below[0][below[1], y] + above[0][above[1], y] + (before + after)
        beside = beside + jnp.where(first, 0.0, pltpu.roll(centre, 1, 1))
        beside = beside + jnp.where(last, 0.0, pltpu.roll(centre, NZ - 1, 1))
        emit(y, coef(y) * centre - weight * beside)
        before, centre = centre, after


def moments(panel, planes):
    def plane_sum(plane, acc):
        for y in range(0, NY, 2):

            def rows(at, size):
                return jnp.concatenate(
                    [panel[plane, y, pl.ds(at, size), :], panel[plane, y + 1, pl.ds(at, size), :]], 1
                )

            ends = [rows(at, NRHS) for at in (0, PIECE, SSTEP * NRHS, PIECE + SSTEP * NRHS)]
            acc = acc + lax.dot_general(
                rows(0, 2 * PIECE),
                jnp.concatenate(ends, 0),
                (((1,), (1,)), ((), ())),
                preferred_element_type=F32,
            )
        return acc

    def body(i, acc):
        return plane_sum(2 * i + 1, plane_sum(2 * i, acc))

    acc = lax.fori_loop(0, planes // 2, body, jnp.zeros((2 * PIECE, 4 * NRHS), F32))
    acc = acc[:PIECE] + acc[PIECE:]
    low = acc[:, :NRHS] + acc[:, NRHS : 2 * NRHS]
    high = acc[:, 2 * NRHS : 3 * NRHS] + acc[:, 3 * NRHS :]
    blocks = [low[j * NRHS : (j + 1) * NRHS] for j in range(KB)]
    blocks += [high[j * NRHS : (j + 1) * NRHS] for j in range(1, SSTEP)]
    return jnp.concatenate(blocks, 1)


def solve(mom):
    size = SSTEP * NRHS
    step = 4
    shifted = jnp.concatenate([mom[:, NRHS:], mom[:, :NRHS]], 1)
    band = SHIFT * mom + SCALE * shifted
    blocks = [band[:, i * NRHS : i * NRHS + size] for i in range(SSTEP)]
    work = jnp.concatenate(blocks + [mom[:, :size]], 0)
    lane = lax.broadcasted_iota(jnp.int32, (1, size), 1)
    sub = lax.broadcasted_iota(jnp.int32, (step, 1), 0)
    for j in range(0, size, step):
        off = j % 8
        if off == 0 and j:
            work = work[8:]
        inside = (lane >= j) & (lane < j + step)
        rows = work[off : off + step]
        cols = [jnp.broadcast_to(rows[:, j + t : j + t + 1], (step, size)) for t in range(step)]
        rows = jnp.where(inside, (lane - j == sub).astype(F32), rows)
        for t in range(step):
            inv = 1.0 / cols[t][t : t + 1]
            factor = jnp.where(sub == t, 0.0, cols[t])

            def eliminate(m):
                row = m[t : t + 1] * inv
                return jnp.where(sub == t, row, m - factor * row)

            rows = eliminate(rows)
            cols = [eliminate(c) if u > t else c for u, c in enumerate(cols)]
        acc = work[:, j : j + 1] * rows[0:1]
        for t in range(1, step):
            acc = acc + work[:, j + t : j + t + 1] * rows[t : t + 1]
        work = jnp.where(inside, acc, work - acc)
    return work[8:]


def coef_rows(coef_t):
    pad = jnp.zeros((NRHS, NRHS), F32)
    eye = (
        lax.broadcasted_iota(jnp.int32, (NRHS, PIECE), 0)
        == lax.broadcasted_iota(jnp.int32, (NRHS, PIECE), 1)
    ).astype(F32)
    same = jnp.concatenate([coef_t, pad], 1)
    up = jnp.concatenate([pad, coef_t], 1)
    left = eye - (SHIFT * same + SCALE * up)
    l_hi, l_mid, l_lo = pieces(left)
    c_hi, c_mid, _ = pieces(same)
    none = jnp.zeros((NRHS, PIECE), BF16)
    rows = [
        [l_hi, l_hi, l_hi],
        [l_mid, l_mid, none],
        [l_lo, none, none],
        [c_hi, c_hi, none],
        [c_mid, none, none],
    ]
    return jnp.concatenate([jnp.concatenate(r, 1) for r in rows], 0)


def combine(coefs, panel, plane, emit):
    for y in range(0, NY, 2):
        block = jnp.concatenate([panel[plane, y], panel[plane, y + 1]], 1)
        out = jnp.dot(coefs, block, preferred_element_type=F32)
        left = out[:NRHS] + out[NRHS : 2 * NRHS] + out[2 * NRHS : 3 * NRHS]
        step = out[3 * NRHS : 4 * NRHS] + out[4 * NRHS :]
        for k in range(2):
            emit(y + k, left[:, k * NZ : (k + 1) * NZ], step[:, k * NZ : (k + 1) * NZ])


def pack_kernel(info, right, diag, near_top, near_first, far_top, far_first, sems):
    count = info[0]
    copies = []
    places = ((near_top, count - SSTEP), (near_first, 0), (far_top, count - 2 * SSTEP), (far_first, SSTEP))
    for i, (out, at) in enumerate(places):
        copies.append(
            pltpu.make_async_copy(
                right.at[:, pl.ds(at, SSTEP)], out.at[pl.ds(0, NRHS)], sems.at[2 * i]
            )
        )
        copies.append(
            pltpu.make_async_copy(diag.at[pl.ds(at, SSTEP)], out.at[NRHS], sems.at[2 * i + 1])
        )
    for copy in copies:
        copy.start()
    for copy in copies:
        copy.wait()


def inner_kernel(info, right, diag, panel, mom, field_0, field_1, field_2, field_3):
    count = info[0]
    rows = NY * CX
    fields = (field_0, field_1, field_2, field_3)

    def load(p):
        for y in range(NY):
            field_0[p, y] = right[pl.Slice(p * NY + y, NRHS, rows), :]

    over(0, CX, load)

    def keep_of(p):
        return (p < count - SSTEP).astype(F32)

    def split(p):
        keep = keep_of(p + SSTEP)
        for y in range(NY):
            store_pieces(panel, p, y, 0, field_0[p + SSTEP, y] * keep)

    over(0, MID, split)
    weight = 1.0 / SCALE
    for power in range(1, SSTEP + 1):
        src = fields[power - 1]

        def apply(p, inner):
            keep = keep_of(p)

            def emit(y, value):
                if power < SSTEP:
                    fields[power][p, y] = value
                if inner:
                    store_pieces(panel, p - SSTEP, y, power, value * keep)

            plane_step(
                (src, p - 1), (src, p), (src, p + 1),
                lambda y: coef_of(diag[p, pl.ds(y, 1), :]), weight, emit,
            )

        for p in range(power, SSTEP):
            apply(p, False)
            apply(CX - 1 - p, False)
        over(SSTEP, CX - SSTEP, lambda p: apply(p, True))
    mom[...] = moments(panel, MID)


def halo_diag(halo, i, y):
    return halo[pl.ds(NRHS * SSTEP * NY + i * NY + y, 1), :]


def edge_kernel(
    info, lower, upper, diag, mom_in, field_0, field_1, field_2, field_3, panel, mom, side_l, side_u
):
    count = info[0]
    fields = (field_0, field_1, field_2, field_3)
    for i in range(SSTEP):
        for y in range(NY):
            side_l[0, i, y] = lower[pl.Slice(i * NY + y, NRHS, SSTEP * NY), :]
            side_u[0, i, y] = upper[pl.Slice((SSTEP - 1 - i) * NY + y, NRHS, SSTEP * NY), :]
    for top in (False, True):
        side, halo = (side_u, upper) if top else (side_l, lower)
        outside = jnp.where(info[2 if top else 1] > 0, 1.0 / SCALE, 0.0).astype(F32)

        def own(q):
            return count - 1 - q if top else q

        for power in range(SSTEP + 1):

            def source(level, q):
                if q <= level - 1:
                    return side.at[level], q - (level - SSTEP)
                return fields[level], own(q)

            for q in range(power, SSTEP):
                split_plane(panel, q + (SSTEP if top else 0), power, fields[power], own(q))
            if power == 0:
                continue
            for q in range(power - SSTEP, power):

                def coef(y):
                    if q >= 0:
                        return coef_of(diag[own(q), pl.ds(y, 1), :])
                    return coef_of(halo_diag(halo, -1 - q if top else q + SSTEP, y))

                def emit(y, value):
                    if power < SSTEP:
                        side[power, q - (power - SSTEP), y] = value
                    if q >= 0:
                        store_pieces(panel, q + (SSTEP if top else 0), y, power, value)

                plane_step(
                    source(power - 1, q - 1), source(power - 1, q), source(power - 1, q + 1),
                    coef, outside if q < 0 else 1.0 / SCALE, emit,
                )
    mom[...] = mom_in[...] + moments(panel, 2 * SSTEP)


def ghost_kernel(
    info, lower, upper, far_lower, far_upper, diag, side_l, side_u, panel, coef, far_a, far_b
):
    count = info[0]
    for i in range(MIDDLE - CX):
        coef[CX + i] = jnp.zeros((NY, NZ), F32)
    for i in range(CX):
        coef[SSTEP + i] = coef_of(diag[i])
    base = NRHS * SSTEP * NY
    for i in range(SSTEP):
        coef[i] = coef_of(lower[pl.ds(base + i * NY, NY), :])
        coef[SSTEP + count + i] = coef_of(upper[pl.ds(base + i * NY, NY), :])
    for top in (False, True):
        side, near, far = (side_u, upper, far_upper) if top else (side_l, lower, far_lower)
        weight = jnp.where(info[2 if top else 1] > 0, 1.0 / SCALE, 0.0).astype(F32)
        shift = SSTEP if top else 0
        for i in range(SSTEP):
            for y in range(NY):
                j = SSTEP - 1 - i if top else i
                far_a[i, y] = far[pl.Slice(j * NY + y, NRHS, SSTEP * NY), :]
        buffers = (far_a, far_b)
        for power in range(SSTEP + 1):
            for q in range(power - SSTEP, 0):
                split_plane(panel, q + SSTEP + shift, power, side.at[power], q - (power - SSTEP))
            if power == 0:
                continue
            src, dst = buffers[(power - 1) % 2], buffers[power % 2]

            def source(q):
                if q <= power - 6:
                    return src, q - (power - 9)
                return side.at[power - 1], q - (power - 5)

            for q in range(power - 8, power - 4):

                def diag_row(y):
                    if q >= -SSTEP:
                        return coef_of(halo_diag(near, -1 - q if top else q + SSTEP, y))
                    return coef_of(halo_diag(far, -5 - q if top else q + 8, y))

                def emit(y, value):
                    if power < SSTEP:
                        dst[q - (power - 8), y] = value
                    if q >= -SSTEP:
                        store_pieces(panel, q + SSTEP + shift, y, power, value)

                plane_step(source(q - 1), source(q), source(q + 1), diag_row, weight, emit)


def middle_kernel(
    info, mom_in, coef, inner, edge, ghost, panel_a, panel_b, mom, iterate, field_a, field_b
):
    count = info[0]
    coefs = coef_rows(solve(mom_in[...]))

    def weight_of(plane):
        inside = (
            ((plane >= SSTEP) | (info[1] > 0))
            & ((plane < SSTEP + count) | (info[2] > 0))
            & (plane < 2 * SSTEP + count)
        )
        return jnp.where(inside, 1.0 / SCALE, 0.0).astype(F32)

    def update(store, plane, at, own):
        def emit(y, left, step):
            field_a[at, y] = left
            if own:
                iterate[at - SSTEP, y] = step

        combine(coefs, store, plane, emit)

    for i in range(MIDDLE - CX):
        field_a[CX + i] = jnp.zeros(FIELD, F32)
    for i in range(SSTEP):
        iterate[CX - SSTEP + i] = jnp.zeros(FIELD, F32)
    over(0, SSTEP, lambda p: update(ghost, p, p, False))
    over(0, SSTEP, lambda p: update(edge, p, p + SSTEP, True))
    over(0, MID, lambda p: update(inner, p, p + 2 * SSTEP, True))
    over(0, SSTEP, lambda p: update(edge, 2 * SSTEP - 1 - p, count + p, True))
    over(0, SSTEP, lambda p: update(ghost, 2 * SSTEP - 1 - p, count + SSTEP + p, False))

    def keep_of(p):
        return (p < SSTEP + count).astype(F32)

    halves = ((panel_a, SSTEP), (panel_b, SSTEP + MID))
    for panel, base in halves:

        def split(p):
            keep = keep_of(p)
            for y in range(NY):
                store_pieces(panel, p - base, y, 0, field_a[p, y] * keep)

        over(base, base + MID, split)
    fields = (field_a, field_b)
    for power in range(1, SSTEP + 1):
        src, dst = fields[(power - 1) % 2], fields[power % 2]

        def apply(p, panel, base):
            keep = keep_of(p)

            def emit(y, value):
                if power < SSTEP:
                    dst[p, y] = value
                if panel is not None:
                    store_pieces(panel, p - base, y, power, value * keep)

            plane_step(
                (src, p - 1), (src, p), (src, p + 1),
                lambda y: coef[p, pl.ds(y, 1), :], weight_of(p), emit,
            )

        for p in range(power, SSTEP):
            apply(p, None, 0)
            apply(MIDDLE - 1 - p, None, 0)
        for panel, base in halves:
            over(base, base + MID, lambda p: apply(p, panel, base))
    mom[...] = moments(panel_a, MID) + moments(panel_b, MID)


def last_kernel(info, mom_in, panel_a, panel_b, iterate, solution_field, residual):
    count = info[0]
    rows = NY * CX
    coefs = coef_rows(solve(mom_in[...]))

    def update(panel, plane, p):
        keep = (p < count).astype(F32)

        def emit(y, left, step):
            at = pl.Slice(p * NY + y, NRHS, rows)
            residual[at, :] = left
            solution_field[at, :] = iterate[p, y] * keep + step

        combine(coefs, panel, plane, emit)

    over(0, MID, lambda p: update(panel_a, p, p))
    over(0, MID, lambda p: update(panel_b, p, p + MID))


SMEM_SPEC = pl.BlockSpec(memory_space=pltpu.SMEM)
VMEM_SPEC = pl.BlockSpec(memory_space=pltpu.VMEM)


def call(body, limit, operands, outs, scratch, kept_operands=(), cost=1, aliases={}):
    operands = [
        pltpu.with_memory_space_constraint(x, pltpu.VMEM) if i in kept_operands else x
        for i, x in enumerate(operands)
    ]
    return pl.pallas_call(
        body,
        out_shape=[pltpu.VMEM(s, d) if kept else jax.ShapeDtypeStruct(s, d) for s, d, kept in outs],
        in_specs=[SMEM_SPEC] + [VMEM_SPEC] * (len(operands) - 1),
        out_specs=[VMEM_SPEC] * len(outs),
        scratch_shapes=scratch,
        input_output_aliases=aliases,
        cost_estimate=pl.CostEstimate(
            flops=cost * 1_000_000_000, bytes_accessed=cost * 3_000_000, transcendentals=0
        ),
        compiler_params=pltpu.CompilerParams(vmem_limit_bytes=limit * 1024 * 1024),
    )(*operands)


def reduce_all(value, size, beside=None):
    if size == 128:
        rounds = [(1, 2), (2, 4), (8, 4), (32, 4)]
    else:
        rounds = [(1 << b, 2) for b in range(size.bit_length() - 1)]
    for place_in_order, (stride, width) in enumerate(rounds):
        total = value
        if beside is not None and place_in_order == 2:
            total, beside = lax.optimization_barrier((total, beside))
        for turn in range(1, width):
            route = []
            for i in range(size):
                place = i // stride % width
                route.append((i, i + ((place + turn) % width - place) * stride))
            total = total + lax.ppermute(value, AXES, route)
        value = total
    return value, beside


def local(right_side, diagonal, counts):
    count = counts[0]
    size = lax.axis_size(AXES)
    me = lax.axis_index(AXES)
    info = jnp.stack([count, me, size - 1 - me]).astype(jnp.int32)

    packed = ((NRHS + 1, SSTEP, NY, NZ), F32, True)
    near_top, near_first, far_top, far_first = pl.pallas_call(
        pack_kernel,
        out_shape=[pltpu.VMEM(packed[0], F32)] * 4,
        in_specs=[SMEM_SPEC] + [pl.BlockSpec(memory_space=pltpu.HBM)] * 2,
        out_specs=[VMEM_SPEC] * 4,
        scratch_shapes=[pltpu.SemaphoreType.DMA((8,))],
        compiler_params=pltpu.CompilerParams(vmem_limit_bytes=8 * 1024 * 1024),
    )(
        info,
        pltpu.with_memory_space_constraint(right_side, pltpu.HBM),
        pltpu.with_memory_space_constraint(diagonal, pltpu.HBM),
    )
    upward = [(i, i + 1) for i in range(size - 1)]
    downward = [(i + 1, i) for i in range(size - 1)]
    halo = ((NRHS + 1) * SSTEP * NY, NZ)
    lower = lax.ppermute(near_top, AXES, upward)
    upper = lax.ppermute(near_first, AXES, downward)
    inner, mom_inner, f0, f1, f2, f3 = call(
        inner_kernel,
        12,
        (info, right_side.reshape(NRHS * CX * NY, NZ), diagonal),
        [((MID,) + PANEL, BF16, True), ((NRHS, NZ), F32, False)]
        + [((CX,) + FIELD, F32, True)] * SSTEP,
        [],
        cost=4,
    )
    lower, upper = lower.reshape(halo), upper.reshape(halo)
    edge, mom, side_l, side_u = call(
        edge_kernel,
        8,
        (info, lower, upper, diagonal, mom_inner, f0, f1, f2, f3),
        [
            ((2 * SSTEP,) + PANEL, BF16, True),
            ((NRHS, NZ), F32, False),
            ((SSTEP, SSTEP) + FIELD, F32, True),
            ((SSTEP, SSTEP) + FIELD, F32, True),
        ],
        [],
        (5, 6, 7, 8),
        cost=4,
    )
    mom, far_top, far_first = lax.optimization_barrier((mom, far_top, far_first))
    far_lower = lax.ppermute(far_top, AXES, upward).reshape(halo)
    far_upper = lax.ppermute(far_first, AXES, downward).reshape(halo)
    ghost, coef = call(
        ghost_kernel,
        8,
        (info, lower, upper, far_lower, far_upper, diagonal, side_l, side_u),
        [((2 * SSTEP,) + PANEL, BF16, True), ((MIDDLE, NY, NZ), F32, True)],
        [pltpu.VMEM((SSTEP,) + FIELD, F32), pltpu.VMEM((SSTEP,) + FIELD, F32)],
        (6, 7),
        cost=3,
    )
    mom, coef = reduce_all(mom, size, coef)
    panel_a, panel_b, mom, iterate = call(
        middle_kernel,
        8,
        (info, mom, coef, inner, edge, ghost),
        [
            ((MID,) + PANEL, BF16, True),
            ((MID,) + PANEL, BF16, True),
            ((NRHS, NZ), F32, False),
            ((CX,) + FIELD, F32, True),
        ],
        [pltpu.VMEM((MIDDLE,) + FIELD, F32), pltpu.VMEM((MIDDLE,) + FIELD, F32)],
        (2, 3, 4, 5),
        cost=10,
        aliases={3: 0, 4: 1},
    )
    mom, _ = reduce_all(mom, size)
    out = (NRHS * CX * NY, NZ)
    solution_field, residual = call(
        last_kernel,
        8,
        (info, mom, panel_a, panel_b, iterate),
        [(out, F32, False), (out, F32, False)],
        [],
        (2, 3, 4),
        cost=4,
    )
    return (solution_field.reshape(right_side.shape), residual.reshape(right_side.shape))


def solution(mesh):
    in_specs = (
        P(None, AXES, None, None),
        P(AXES, None, None),
        P(AXES),
    )
    out_specs = (P(None, AXES, None, None), P(None, AXES, None, None))
    return jax.shard_map(local, mesh=mesh, in_specs=in_specs, out_specs=out_specs, check_vma=False)
```

```python
import jax
import jax.numpy as jnp
from jax import lax
from jax.experimental import pallas as pl
from jax.experimental.pallas import tpu as pltpu
from jax.sharding import PartitionSpec as P

NRHS = 16
SSTEP = 4
SHIFT = 8.5
SCALE = 7.5
CX = 16
NY = 16
NZ = 128
KB = SSTEP + 1
PIECE = KB * NRHS
MID = CX - 2 * SSTEP
MIDDLE = CX + 2 * SSTEP
AXES = ("grp", "dom")
F32 = jnp.float32
BF16 = jnp.bfloat16
FIELD = (NY, NRHS, NZ)
PANEL = (NY, 3 * PIECE, NZ)


def over(start, stop, body, group=4):
    whole = (stop - start) // group

    def step(i, carry):
        for k in range(group):
            body(start + i * group + k)
        return carry

    if whole:
        lax.fori_loop(0, whole, step, 0)
    for plane in range(start + whole * group, stop):
        body(plane)


def pieces(value):
    hi = value.astype(BF16)
    rest = value - hi.astype(F32)
    mid = rest.astype(BF16)
    lo = (rest - mid.astype(F32)).astype(BF16)
    return hi, mid, lo


def store_pieces(panel, plane, y, power, value):
    for i, part in enumerate(pieces(value)):
        panel[plane, y, pl.ds(i * PIECE + power * NRHS, NRHS), :] = part


def split_plane(panel, at, power, field, plane):
    for y in range(NY):
        store_pieces(panel, at, y, power, field[plane, y])


def coef_of(diag):
    return (diag + (6.0 - SHIFT)) * (1.0 / SCALE)


def plane_step(below, centre_at, above, coef, weight, emit):
    lane = lax.broadcasted_iota(jnp.int32, (NRHS, NZ), 1)
    first = lane == 0
    last = lane == NZ - 1
    zero = jnp.zeros((NRHS, NZ), F32)
    src, plane = centre_at
    before = zero
    centre = src[plane, 0]
    for y in range(NY):
        after = src[plane, y + 1] if y + 1 < NY else zero
        beside = below[0][below[1], y] + above[0][above[1], y] + (before + after)
        beside = beside + jnp.where(first, 0.0, pltpu.roll(centre, 1, 1))
        beside = beside + jnp.where(last, 0.0, pltpu.roll(centre, NZ - 1, 1))
        emit(y, coef(y) * centre - weight * beside)
        before, centre = centre, after


def moment_sum(panel, plane, acc):
    for y in range(0, NY, 2):

        def rows(at, size):
            return jnp.concatenate(
                [panel[plane, y, pl.ds(at, size), :], panel[plane, y + 1, pl.ds(at, size), :]], 1
            )

        ends = [rows(at, NRHS) for at in (0, PIECE, SSTEP * NRHS, PIECE + SSTEP * NRHS)]
        acc = acc + lax.dot_general(
            rows(0, 2 * PIECE),
            jnp.concatenate(ends, 0),
            (((1,), (1,)), ((), ())),
            preferred_element_type=F32,
        )
    return acc


def moment_zero():
    return jnp.zeros((2 * PIECE, 4 * NRHS), F32)


def moment_blocks(acc):
    acc = acc[:PIECE] + acc[PIECE:]
    low = acc[:, :NRHS] + acc[:, NRHS : 2 * NRHS]
    high = acc[:, 2 * NRHS : 3 * NRHS] + acc[:, 3 * NRHS :]
    blocks = [low[j * NRHS : (j + 1) * NRHS] for j in range(KB)]
    blocks += [high[j * NRHS : (j + 1) * NRHS] for j in range(1, SSTEP)]
    return jnp.concatenate(blocks, 1)


def inverse4(m):
    def inverse2(a, b, d):
        scale = 1.0 / (a * d - b * b)
        return d * scale, -b * scale, a * scale

    p, q, r = inverse2(m[0][0], m[0][1], m[1][1])
    f00, f01 = p * m[0][2] + q * m[1][2], p * m[0][3] + q * m[1][3]
    f10, f11 = q * m[0][2] + r * m[1][2], q * m[0][3] + r * m[1][3]
    a = m[2][2] - (m[0][2] * f00 + m[1][2] * f10)
    b = m[2][3] - (m[0][2] * f01 + m[1][2] * f11)
    d = m[3][3] - (m[0][3] * f01 + m[1][3] * f11)
    u, v, w = inverse2(a, b, d)
    g00, g01 = f00 * u + f01 * v, f00 * v + f01 * w
    g10, g11 = f10 * u + f11 * v, f10 * v + f11 * w
    x00 = p + (g00 * f00 + g01 * f01)
    x01 = q + (g00 * f10 + g01 * f11)
    x11 = r + (g10 * f10 + g11 * f11)
    return [
        [x00, x01, -g00, -g01],
        [x01, x11, -g10, -g11],
        [-g00, -g10, u, v],
        [-g01, -g11, v, w],
    ]


def solve(mom):
    size = SSTEP * NRHS
    step = 4
    shifted = jnp.concatenate([mom[:, NRHS:], mom[:, :NRHS]], 1)
    band = SHIFT * mom + SCALE * shifted
    blocks = [band[:, i * NRHS : i * NRHS + size] for i in range(SSTEP)]
    work = jnp.concatenate(blocks + [mom[:, :size]], 0)
    lane = lax.broadcasted_iota(jnp.int32, (1, size), 1)
    for j in range(0, size, step):
        off = j % 8
        if off == 0 and j:
            work = work[8:]
        inside = (lane >= j) & (lane < j + step)
        rows = work[off : off + step]
        cols = [jnp.broadcast_to(rows[:, j + t : j + t + 1], (step, size)) for t in range(step)]
        inverse = inverse4([[cols[t][s : s + 1] for t in range(step)] for s in range(step)])
        new = []
        for s in range(step):
            row = inverse[s][0] * rows[0:1]
            unit = inverse[s][0]
            for t in range(1, step):
                row = row + inverse[s][t] * rows[t : t + 1]
                unit = jnp.where(lane == j + t, inverse[s][t], unit)
            new.append(jnp.where(inside, unit, row))
        acc = work[:, j : j + 1] * new[0]
        for t in range(1, step):
            acc = acc + work[:, j + t : j + t + 1] * new[t]
        work = jnp.where(inside, acc, work - acc)
    return work[8:]


def coef_rows(coef_t):
    pad = jnp.zeros((NRHS, NRHS), F32)
    eye = (
        lax.broadcasted_iota(jnp.int32, (NRHS, PIECE), 0)
        == lax.broadcasted_iota(jnp.int32, (NRHS, PIECE), 1)
    ).astype(F32)
    same = jnp.concatenate([coef_t, pad], 1)
    up = jnp.concatenate([pad, coef_t], 1)
    left = eye - (SHIFT * same + SCALE * up)
    l_hi, l_mid, l_lo = pieces(left)
    c_hi, c_mid, _ = pieces(same)
    none = jnp.zeros((NRHS, PIECE), BF16)
    rows = [
        [l_hi, l_hi, l_hi],
        [l_mid, l_mid, none],
        [l_lo, none, none],
        [c_hi, c_hi, none],
        [c_mid, none, none],
    ]
    return jnp.concatenate([jnp.concatenate(r, 1) for r in rows], 0)


def combine(coefs, panel, plane, emit):
    for y in range(0, NY, 2):
        block = jnp.concatenate([panel[plane, y], panel[plane, y + 1]], 1)
        out = jnp.dot(coefs, block, preferred_element_type=F32)
        left = out[:NRHS] + out[NRHS : 2 * NRHS] + out[2 * NRHS : 3 * NRHS]
        step = out[3 * NRHS : 4 * NRHS] + out[4 * NRHS :]
        for k in range(2):
            emit(y + k, left[:, k * NZ : (k + 1) * NZ], step[:, k * NZ : (k + 1) * NZ])


def pack(right, diag, places, sems):
    copies = []
    for i, (out, at) in enumerate(places):
        copies.append(
            pltpu.make_async_copy(
                right.at[:, pl.ds(at, SSTEP)], out.at[pl.ds(0, NRHS)], sems.at[2 * i]
            )
        )
        copies.append(
            pltpu.make_async_copy(diag.at[pl.ds(at, SSTEP)], out.at[NRHS], sems.at[2 * i + 1])
        )
    for copy in copies:
        copy.start()
    return copies


def pack_kernel(info, right, diag, near_same, near_next, far_same, far_next, sems):
    count = info[0]
    even = info[1] % 2 == 0
    places = (
        (near_same, jnp.where(even, count - SSTEP, 0)),
        (near_next, jnp.where(even, 0, count - SSTEP)),
        (far_same, jnp.where(even, count - 2 * SSTEP, SSTEP)),
        (far_next, jnp.where(even, SSTEP, count - 2 * SSTEP)),
    )
    for copy in pack(right, diag, places, sems):
        copy.wait()


def inner_kernel(info, right, diag, panel, mom, field_0, field_1, field_2, field_3):
    count = info[0]
    rows = NY * CX
    fields = (field_0, field_1, field_2, field_3)

    def load(p):
        for y in range(NY):
            field_0[p, y] = right[pl.Slice(p * NY + y, NRHS, rows), :]

    over(0, CX, load)

    def keep_of(p):
        return (p < count - SSTEP).astype(F32)

    def split(p):
        keep = keep_of(p + SSTEP)
        for y in range(NY):
            store_pieces(panel, p + SSTEP, y, 0, field_0[p + SSTEP, y] * keep)

    over(0, MID, split)
    weight = 1.0 / SCALE
    for power in range(1, SSTEP + 1):
        src = fields[power - 1]

        def apply(p, inner):
            keep = keep_of(p)

            def emit(y, value):
                if power < SSTEP:
                    fields[power][p, y] = value
                if inner:
                    store_pieces(panel, p, y, power, value * keep)

            plane_step(
                (src, p - 1), (src, p), (src, p + 1),
                lambda y: coef_of(diag[p, pl.ds(y, 1), :]), weight, emit,
            )

        for p in range(power, SSTEP):
            apply(p, False)
            apply(CX - 1 - p, False)
        over(SSTEP, CX - SSTEP, lambda p: apply(p, True))

    def two(i, acc):
        return moment_sum(panel, SSTEP + 2 * i + 1, moment_sum(panel, SSTEP + 2 * i, acc))

    mom[...] = moment_blocks(lax.fori_loop(0, MID // 2, two, moment_zero()))


def load_halo(info, same, following, field_l, field_u, diags):
    even = info[1] % 2 == 0

    def pick(at):
        a, b = same[at, :], following[at, :]
        return jnp.where(even, b, a), jnp.where(even, a, b)

    for i in range(SSTEP):
        for y in range(NY):
            low, high = pick(pl.Slice(i * NY + y, NRHS, SSTEP * NY))
            field_l[i, y] = low
            field_u[SSTEP - 1 - i, y] = high
        low, high = pick(pl.ds((NRHS * SSTEP + i) * NY, NY))
        diags[i] = low
        diags[SSTEP + i] = high


def edge_kernel(
    info, same, following, diag, mom_in, field_0, field_1, field_2, field_3, panel_in,
    panel, mom, side_l, side_u, diags,
):
    count = info[0]
    fields = (field_0, field_1, field_2, field_3)
    acc = moment_zero()
    load_halo(info, same, following, side_l.at[0], side_u.at[0], diags)
    for top in (False, True):
        side = side_u if top else side_l
        outside = jnp.where(info[2 if top else 1] > 0, 1.0 / SCALE, 0.0).astype(F32)

        def own(q):
            return count - 1 - q if top else q

        def slot(q):
            return CX - 1 - q if top else q

        for power in range(SSTEP + 1):

            def source(level, q):
                if q <= level - 1:
                    return side.at[level], q - (level - SSTEP)
                return fields[level], own(q)

            for q in range(power, SSTEP):
                split_plane(panel, slot(q), power, fields[power], own(q))
            if power == 0:
                continue
            for q in range(power - SSTEP, power):

                def coef(y):
                    if q >= 0:
                        return coef_of(diag[own(q), pl.ds(y, 1), :])
                    return coef_of(diags[SSTEP - 1 - q if top else q + SSTEP, pl.ds(y, 1), :])

                def emit(y, value):
                    if power < SSTEP:
                        side[power, q - (power - SSTEP), y] = value
                    if q >= 0:
                        store_pieces(panel, slot(q), y, power, value)

                plane_step(
                    source(power - 1, q - 1), source(power - 1, q), source(power - 1, q + 1),
                    coef, outside if q < 0 else 1.0 / SCALE, emit,
                )
            if top:
                acc = moment_sum(panel, power - 1, acc)
    for q in range(SSTEP):
        acc = moment_sum(panel, CX - 1 - q, acc)
    mom[...] = mom_in[...] + moment_blocks(acc)


def ghost_kernel(
    info, same, following, diag, diags, side_l, side_u, panel, coef, far_l, far_u, far_b, far_diags
):
    count = info[0]
    for i in range(MIDDLE - CX):
        coef[CX + i] = jnp.zeros((NY, NZ), F32)
    for i in range(CX):
        coef[SSTEP + i] = coef_of(diag[i])
    for i in range(SSTEP):
        coef[i] = coef_of(diags[i])
        coef[SSTEP + count + i] = coef_of(diags[SSTEP + i])
    load_halo(info, same, following, far_l, far_u, far_diags)
    for top in (False, True):
        side, far_a = (side_u, far_u) if top else (side_l, far_l)
        weight = jnp.where(info[2 if top else 1] > 0, 1.0 / SCALE, 0.0).astype(F32)
        shift = SSTEP if top else 0
        buffers = (far_a, far_b)
        for power in range(SSTEP + 1):
            for q in range(power - SSTEP, 0):
                split_plane(panel, q + SSTEP + shift, power, side.at[power], q - (power - SSTEP))
            if power == 0:
                continue
            src, dst = buffers[(power - 1) % 2], buffers[power % 2]

            def source(q):
                if q <= power - 6:
                    return src, q - (power - 9)
                return side.at[power - 1], q - (power - 5)

            for q in range(power - 8, power - 4):

                def diag_row(y):
                    if q >= -SSTEP:
                        return coef_of(diags[SSTEP - 1 - q if top else q + SSTEP, pl.ds(y, 1), :])
                    return coef_of(far_diags[-1 - q if top else q + 2 * SSTEP, pl.ds(y, 1), :])

                def emit(y, value):
                    if power < SSTEP:
                        dst[q - (power - 8), y] = value
                    if q >= -SSTEP:
                        store_pieces(panel, q + SSTEP + shift, y, power, value)

                plane_step(source(q - 1), source(q), source(q + 1), diag_row, weight, emit)


def middle_kernel(
    info, mom_in, coef, panel_in, ghost, panel, mom, iterate, field_0, field_1, field_2, field_3
):
    count = info[0]
    coefs = coef_rows(solve(mom_in[...]))

    def weight_of(plane):
        inside = (
            ((plane >= SSTEP) | (info[1] > 0))
            & ((plane < SSTEP + count) | (info[2] > 0))
            & (plane < 2 * SSTEP + count)
        )
        return jnp.where(inside, 1.0 / SCALE, 0.0).astype(F32)

    def update(store, plane, at, own):
        def emit(y, left, step):
            field_0[at, y] = left
            if own:
                iterate[at - SSTEP, y] = step

        combine(coefs, store, plane, emit)

    for i in range(MIDDLE - CX):
        field_0[CX + i] = jnp.zeros(FIELD, F32)
    for i in range(SSTEP):
        iterate[CX - SSTEP + i] = jnp.zeros(FIELD, F32)
    over(0, SSTEP, lambda p: update(ghost, p, p, False))
    over(0, CX - SSTEP, lambda p: update(panel_in, p, p + SSTEP, True))
    over(0, SSTEP, lambda p: update(panel_in, CX - SSTEP + p, count + p, True))
    over(0, SSTEP, lambda p: update(ghost, 2 * SSTEP - 1 - p, count + SSTEP + p, False))
    fields = (field_0, field_1, field_2, field_3)

    def keep_of(p):
        return (p < SSTEP + count).astype(F32)

    def apply(power, p, own):
        src = fields[power - 1]
        keep = keep_of(p)
        if own and power == 1:
            for y in range(NY):
                store_pieces(panel, p - SSTEP, y, 0, src[p, y] * keep)

        def emit(y, value):
            if power < SSTEP:
                fields[power][p, y] = value
            if own:
                store_pieces(panel, p - SSTEP, y, power, value * keep)

        plane_step(
            (src, p - 1), (src, p), (src, p + 1),
            lambda y: coef[p, pl.ds(y, 1), :], weight_of(p), emit,
        )

    def step(p, acc):
        acc = moment_sum(panel, p - 7 - SSTEP, acc)
        for power in range(SSTEP, 0, -1):
            apply(power, p - 2 * (power - 1), True)
        return acc

    def partial_step(p, acc):
        if SSTEP <= p - 7 < SSTEP + CX:
            acc = moment_sum(panel, p - 7 - SSTEP, acc)
        for power in range(SSTEP, 0, -1):
            q = p - 2 * (power - 1)
            if power <= q < MIDDLE - power:
                apply(power, q, SSTEP <= q < SSTEP + CX)
        return acc

    acc = moment_zero()
    for p in range(1, 11):
        acc = partial_step(p, acc)
    acc = lax.fori_loop(11, 20, step, acc)
    for p in range(20, 27):
        acc = partial_step(p, acc)
    mom[...] = moment_blocks(acc)


def last_kernel(info, mom_in, panel, iterate, solution_field, residual, new_field, new_residual, sems):
    rows = NY * CX
    group = 4
    coefs = coef_rows(solve(mom_in[...]))

    def copies(i):
        planes = pl.ds(i * group, group)
        return [
            pltpu.make_async_copy(new_field.at[:, planes], solution_field.at[:, planes], sems.at[0, i]),
            pltpu.make_async_copy(new_residual.at[:, planes], residual.at[:, planes], sems.at[1, i]),
        ]

    flat = NRHS * rows, NZ
    flat_field, flat_residual = new_field.reshape(flat), new_residual.reshape(flat)

    def body(i, carry):
        for k in range(group):
            p = i * group + k

            def emit(y, left, step):
                at = pl.Slice(p * NY + y, NRHS, rows)
                flat_residual[at, :] = left
                flat_field[at, :] = iterate[p, y] + step

            combine(coefs, panel, p, emit)
        for copy in copies(i):
            copy.start()
        return carry

    lax.fori_loop(0, CX // group, body, 0)
    for i in range(CX // group):
        for copy in copies(i):
            copy.wait()


SMEM_SPEC = pl.BlockSpec(memory_space=pltpu.SMEM)
VMEM_SPEC = pl.BlockSpec(memory_space=pltpu.VMEM)
HBM_SPEC = pl.BlockSpec(memory_space=pltpu.HBM)


def call(body, limit, operands, outs, scratch, kept_operands=(), far_operands=(), cost=1, aliases={}):
    operands = [
        pltpu.with_memory_space_constraint(x, pltpu.VMEM)
        if i in kept_operands
        else pltpu.with_memory_space_constraint(x, pltpu.HBM)
        if i in far_operands
        else x
        for i, x in enumerate(operands)
    ]
    return pl.pallas_call(
        body,
        out_shape=[pltpu.VMEM(s, d) if kept else jax.ShapeDtypeStruct(s, d) for s, d, kept in outs],
        in_specs=[SMEM_SPEC]
        + [HBM_SPEC if i in far_operands else VMEM_SPEC for i in range(1, len(operands))],
        out_specs=[VMEM_SPEC if kept is not None else HBM_SPEC for _, _, kept in outs],
        scratch_shapes=scratch,
        input_output_aliases=aliases,
        cost_estimate=pl.CostEstimate(
            flops=cost * 1_000_000_000, bytes_accessed=cost * 3_000_000, transcendentals=0
        ),
        compiler_params=pltpu.CompilerParams(vmem_limit_bytes=limit * 1024 * 1024),
    )(*operands)


def reduce_all(value, size, beside=None):
    if size == 128:
        rounds = [(1, 2), (2, 4), (8, 4), (32, 4)]
    else:
        rounds = [(1 << b, 2) for b in range(size.bit_length() - 1)]
    for place_in_order, (stride, width) in enumerate(rounds):
        total = value
        if beside is not None and place_in_order == 2:
            total, beside = lax.optimization_barrier((total, beside))
        for turn in range(1, width):
            route = []
            for i in range(size):
                place = i // stride % width
                route.append((i, i + ((place + turn) % width - place) * stride))
            total = total + lax.ppermute(value, AXES, route)
        value = total
    return value, beside


def local(right_side, diagonal, counts):
    count = counts[0]
    size = lax.axis_size(AXES)
    me = lax.axis_index(AXES)
    info = jnp.stack([count, me, size - 1 - me]).astype(jnp.int32)

    packed = ((NRHS + 1, SSTEP, NY, NZ), F32, True)
    panel_shape = ((CX,) + PANEL, BF16, True)
    near_same, near_next, far_same, far_next = call(
        pack_kernel,
        4,
        (info, right_side, diagonal),
        [packed] * 4,
        [pltpu.SemaphoreType.DMA((8,))],
        far_operands=(1, 2),
    )
    same = [(i, i ^ 1) for i in range(size)]
    following = [(i, i + 1) for i in range(1, size - 1, 2)] + [(i + 1, i) for i in range(1, size - 1, 2)]
    halo = ((NRHS + 1) * SSTEP * NY, NZ)
    next_halo = lax.ppermute(near_next, AXES, following).reshape(halo)
    same_halo = lax.ppermute(near_same, AXES, same).reshape(halo)
    panel, mom_inner, f0, f1, f2, f3 = call(
        inner_kernel,
        8,
        (info, right_side.reshape(NRHS * CX * NY, NZ), diagonal),
        [panel_shape, ((NRHS, NZ), F32, False)] + [((CX,) + FIELD, F32, True)] * SSTEP,
        [],
        cost=4,
    )
    panel, mom, side_l, side_u, diags = call(
        edge_kernel,
        8,
        (info, same_halo, next_halo, diagonal, mom_inner, f0, f1, f2, f3, panel),
        [
            panel_shape,
            ((NRHS, NZ), F32, False),
            ((SSTEP, SSTEP) + FIELD, F32, True),
            ((SSTEP, SSTEP) + FIELD, F32, True),
            ((2 * SSTEP, NY, NZ), F32, True),
        ],
        [],
        (5, 6, 7, 8, 9),
        cost=4,
        aliases={9: 0},
    )
    mom, far_next, far_same = lax.optimization_barrier((mom, far_next, far_same))
    far_next = lax.ppermute(far_next, AXES, following).reshape(halo)
    far_same = lax.ppermute(far_same, AXES, same).reshape(halo)
    ghost, coef = call(
        ghost_kernel,
        8,
        (info, far_same, far_next, diagonal, diags, side_l, side_u),
        [((2 * SSTEP,) + PANEL, BF16, True), ((MIDDLE, NY, NZ), F32, True)],
        [pltpu.VMEM((SSTEP,) + FIELD, F32)] * 3 + [pltpu.VMEM((2 * SSTEP, NY, NZ), F32)],
        (4, 5, 6),
        cost=3,
    )
    mom, coef = reduce_all(mom, size, coef)
    panel, mom, iterate = call(
        middle_kernel,
        16,
        (info, mom, coef, panel, ghost),
        [
            panel_shape,
            ((NRHS, NZ), F32, False),
            ((CX,) + FIELD, F32, True),
        ],
        [pltpu.VMEM((MIDDLE,) + FIELD, F32)] * SSTEP,
        (2, 3, 4),
        cost=10,
        aliases={3: 0},
    )
    mom, _ = reduce_all(mom, size)
    shape = right_side.shape
    solution_field, residual = call(
        last_kernel,
        8,
        (info, mom, panel, iterate),
        [(shape, F32, None), (shape, F32, None)],
        [pltpu.VMEM(shape, F32), pltpu.VMEM(shape, F32), pltpu.SemaphoreType.DMA((2, CX // 4))],
        (2, 3),
        cost=4,
    )
    return (solution_field, residual)


def solution(mesh):
    in_specs = (
        P(None, AXES, None, None),
        P(AXES, None, None),
        P(AXES),
    )
    out_specs = (P(None, AXES, None, None), P(None, AXES, None, None))
    return jax.shard_map(local, mesh=mesh, in_specs=in_specs, out_specs=out_specs, check_vma=False)
```

```python
import functools

import jax
import jax.numpy as jnp
from jax import lax
from jax.experimental import pallas as pl
from jax.experimental.pallas import tpu as pltpu
from jax.sharding import PartitionSpec as P

NRHS = 16
SSTEP = 4
SHIFT = 8.5
SCALE = 7.5
CX = 16
NY = 16
NZ = 128
KB = SSTEP + 1
PIECE = KB * NRHS
ROUNDS = ((1, 2), (32, 4), (8, 4), (2, 4))
MID = CX - 2 * SSTEP
MIDDLE = CX + 2 * SSTEP
AXES = ("grp", "dom")
F32 = jnp.float32
BF16 = jnp.bfloat16
FIELD = (NY, NRHS, NZ)
PANEL = (NY, 3 * PIECE, NZ)


def over(start, stop, body, group=4):
    whole = (stop - start) // group

    def step(i, carry):
        for k in range(group):
            body(start + i * group + k)
        return carry

    if whole:
        lax.fori_loop(0, whole, step, 0)
    for plane in range(start + whole * group, stop):
        body(plane)


def pieces(value):
    hi = value.astype(BF16)
    rest = value - hi.astype(F32)
    mid = rest.astype(BF16)
    lo = (rest - mid.astype(F32)).astype(BF16)
    return hi, mid, lo


def store_pieces(panel, plane, y, power, value):
    for i, part in enumerate(pieces(value)):
        panel[plane, y, pl.ds(i * PIECE + power * NRHS, NRHS), :] = part


def split_plane(panel, at, power, field, plane):
    for y in range(NY):
        store_pieces(panel, at, y, power, field[plane, y])


def coef_of(diag):
    return (diag + (6.0 - SHIFT)) * (1.0 / SCALE)


def plane_step(below, centre_at, above, coef, weight, emit):
    lane = lax.broadcasted_iota(jnp.int32, (NRHS, NZ), 1)
    first = lane == 0
    last = lane == NZ - 1
    zero = jnp.zeros((NRHS, NZ), F32)
    src, plane = centre_at
    before = zero
    centre = src[plane, 0]
    for y in range(NY):
        after = src[plane, y + 1] if y + 1 < NY else zero
        beside = below[0][below[1], y] + above[0][above[1], y] + (before + after)
        beside = beside + jnp.where(first, 0.0, pltpu.roll(centre, 1, 1))
        beside = beside + jnp.where(last, 0.0, pltpu.roll(centre, NZ - 1, 1))
        emit(y, coef(y) * centre - weight * beside)
        before, centre = centre, after


def moment_sum(panel, plane, acc):
    for y in range(0, NY, 2):

        def rows(at, size):
            return jnp.concatenate(
                [panel[plane, y, pl.ds(at, size), :], panel[plane, y + 1, pl.ds(at, size), :]], 1
            )

        ends = [rows(at, NRHS) for at in (0, PIECE, SSTEP * NRHS, PIECE + SSTEP * NRHS)]
        acc = acc + lax.dot_general(
            rows(0, 2 * PIECE),
            jnp.concatenate(ends, 0),
            (((1,), (1,)), ((), ())),
            preferred_element_type=F32,
        )
    return acc


def moment_zero():
    return jnp.zeros((2 * PIECE, 4 * NRHS), F32)


def moment_blocks(acc):
    acc = acc[:PIECE] + acc[PIECE:]
    low = acc[:, :NRHS] + acc[:, NRHS : 2 * NRHS]
    high = acc[:, 2 * NRHS : 3 * NRHS] + acc[:, 3 * NRHS :]
    blocks = [low[j * NRHS : (j + 1) * NRHS] for j in range(KB)]
    blocks += [high[j * NRHS : (j + 1) * NRHS] for j in range(1, SSTEP)]
    return jnp.concatenate(blocks, 1)


def inverse4(m):
    def inverse2(a, b, d):
        scale = 1.0 / (a * d - b * b)
        return d * scale, -b * scale, a * scale

    p, q, r = inverse2(m[0][0], m[0][1], m[1][1])
    f00, f01 = p * m[0][2] + q * m[1][2], p * m[0][3] + q * m[1][3]
    f10, f11 = q * m[0][2] + r * m[1][2], q * m[0][3] + r * m[1][3]
    a = m[2][2] - (m[0][2] * f00 + m[1][2] * f10)
    b = m[2][3] - (m[0][2] * f01 + m[1][2] * f11)
    d = m[3][3] - (m[0][3] * f01 + m[1][3] * f11)
    u, v, w = inverse2(a, b, d)
    g00, g01 = f00 * u + f01 * v, f00 * v + f01 * w
    g10, g11 = f10 * u + f11 * v, f10 * v + f11 * w
    x00 = p + (g00 * f00 + g01 * f01)
    x01 = q + (g00 * f10 + g01 * f11)
    x11 = r + (g10 * f10 + g11 * f11)
    return [
        [x00, x01, -g00, -g01],
        [x01, x11, -g10, -g11],
        [-g00, -g10, u, v],
        [-g01, -g11, v, w],
    ]


def solve(mom):
    size = SSTEP * NRHS
    step = 4
    shifted = jnp.concatenate([mom[:, NRHS:], mom[:, :NRHS]], 1)
    band = SHIFT * mom + SCALE * shifted
    blocks = [band[:, i * NRHS : i * NRHS + size] for i in range(SSTEP)]
    work = jnp.concatenate(blocks + [mom[:, :size]], 0)
    lane = lax.broadcasted_iota(jnp.int32, (1, size), 1)
    for j in range(0, size, step):
        off = j % 8
        if off == 0 and j:
            work = work[8:]
        inside = (lane >= j) & (lane < j + step)
        rows = work[off : off + step]
        cols = [jnp.broadcast_to(rows[:, j + t : j + t + 1], (step, size)) for t in range(step)]
        inverse = inverse4([[cols[t][s : s + 1] for t in range(step)] for s in range(step)])
        new = []
        for s in range(step):
            row = inverse[s][0] * rows[0:1]
            unit = inverse[s][0]
            for t in range(1, step):
                row = row + inverse[s][t] * rows[t : t + 1]
                unit = jnp.where(lane == j + t, inverse[s][t], unit)
            new.append(jnp.where(inside, unit, row))
        acc = work[:, j : j + 1] * new[0]
        for t in range(1, step):
            acc = acc + work[:, j + t : j + t + 1] * new[t]
        work = jnp.where(inside, acc, work - acc)
    return work[8:]


def coef_rows(coef_t):
    pad = jnp.zeros((NRHS, NRHS), F32)
    eye = (
        lax.broadcasted_iota(jnp.int32, (NRHS, PIECE), 0)
        == lax.broadcasted_iota(jnp.int32, (NRHS, PIECE), 1)
    ).astype(F32)
    same = jnp.concatenate([coef_t, pad], 1)
    up = jnp.concatenate([pad, coef_t], 1)
    left = eye - (SHIFT * same + SCALE * up)
    l_hi, l_mid, l_lo = pieces(left)
    c_hi, c_mid, _ = pieces(same)
    none = jnp.zeros((NRHS, PIECE), BF16)
    rows = [
        [l_hi, l_hi, l_hi],
        [l_mid, l_mid, none],
        [l_lo, none, none],
        [c_hi, c_hi, none],
        [c_mid, none, none],
    ]
    return jnp.concatenate([jnp.concatenate(r, 1) for r in rows], 0)


def combine(coefs, panel, plane, emit):
    for y in range(0, NY, 2):
        block = jnp.concatenate([panel[plane, y], panel[plane, y + 1]], 1)
        out = jnp.dot(coefs, block, preferred_element_type=F32)
        left = out[:NRHS] + out[NRHS : 2 * NRHS] + out[2 * NRHS : 3 * NRHS]
        step = out[3 * NRHS : 4 * NRHS] + out[4 * NRHS :]
        for k in range(2):
            emit(y + k, left[:, k * NZ : (k + 1) * NZ], step[:, k * NZ : (k + 1) * NZ])


def pack(right, diag, places, sems):
    copies = []
    for i, (out, at) in enumerate(places):
        copies.append(
            pltpu.make_async_copy(
                right.at[:, pl.ds(at, SSTEP)], out.at[pl.ds(0, NRHS)], sems.at[2 * i]
            )
        )
        copies.append(
            pltpu.make_async_copy(diag.at[pl.ds(at, SSTEP)], out.at[NRHS], sems.at[2 * i + 1])
        )
    for copy in copies:
        copy.start()
    return copies


def pack_kernel(info, right, diag, near_same, near_next, far_same, far_next, sems):
    count = info[0]
    even = info[1] % 2 == 0
    places = (
        (near_same, jnp.where(even, count - SSTEP, 0)),
        (near_next, jnp.where(even, 0, count - SSTEP)),
        (far_same, jnp.where(even, count - 2 * SSTEP, SSTEP)),
        (far_next, jnp.where(even, SSTEP, count - 2 * SSTEP)),
    )
    for copy in pack(right, diag, places, sems):
        copy.wait()


def inner_kernel(info, right, diag, panel, mom, field_0, field_1, field_2, field_3):
    count = info[0]
    rows = NY * CX
    fields = (field_0, field_1, field_2, field_3)

    def load(p):
        for y in range(NY):
            field_0[p, y] = right[pl.Slice(p * NY + y, NRHS, rows), :]

    over(0, CX, load)

    def keep_of(p):
        return (p < count - SSTEP).astype(F32)

    def split(p):
        keep = keep_of(p + SSTEP)
        for y in range(NY):
            store_pieces(panel, p + SSTEP, y, 0, field_0[p + SSTEP, y] * keep)

    over(0, MID, split)
    weight = 1.0 / SCALE
    for power in range(1, SSTEP + 1):
        src = fields[power - 1]

        def apply(p, inner):
            keep = keep_of(p)

            def emit(y, value):
                if power < SSTEP:
                    fields[power][p, y] = value
                if inner:
                    store_pieces(panel, p, y, power, value * keep)

            plane_step(
                (src, p - 1), (src, p), (src, p + 1),
                lambda y: coef_of(diag[p, pl.ds(y, 1), :]), weight, emit,
            )

        for p in range(power, SSTEP):
            apply(p, False)
            apply(CX - 1 - p, False)
        over(SSTEP, CX - SSTEP, lambda p: apply(p, True))

    def two(i, acc):
        return moment_sum(panel, SSTEP + 2 * i + 1, moment_sum(panel, SSTEP + 2 * i, acc))

    mom[...] = moment_blocks(lax.fori_loop(0, MID // 2, two, moment_zero()))


def load_halo(info, same, following, field_l, field_u, diags):
    even = info[1] % 2 == 0

    def pick(at, top):
        return jnp.where(even, same[at, :], following[at, :]) if top else jnp.where(
            even, following[at, :], same[at, :]
        )

    for top, field in ((False, field_l), (True, field_u)):
        if field is None:
            continue
        for i in range(SSTEP):
            for y in range(NY):
                at = pl.Slice(i * NY + y, NRHS, SSTEP * NY)
                field[SSTEP - 1 - i if top else i, y] = pick(at, top)
            diags[i + SSTEP if top else i] = pick(pl.ds((NRHS * SSTEP + i) * NY, NY), top)


def edge_kernel(
    info, same, following, diag, mom_in, field_0, field_1, field_2, field_3, panel_in,
    panel, mom, side_l, side_u, diags,
):
    count = info[0]
    fields = (field_0, field_1, field_2, field_3)
    acc = moment_zero()
    load_halo(info, same, following, side_l.at[0], side_u.at[0], diags)
    for top in (False, True):
        side = side_u if top else side_l
        outside = jnp.where(info[2 if top else 1] > 0, 1.0 / SCALE, 0.0).astype(F32)

        def own(q):
            return count - 1 - q if top else q

        def slot(q):
            return CX - 1 - q if top else q

        for power in range(SSTEP + 1):

            def source(level, q):
                if q <= level - 1:
                    return side.at[level], q - (level - SSTEP)
                return fields[level], own(q)

            for q in range(power, SSTEP):
                split_plane(panel, slot(q), power, fields[power], own(q))
            if power == 0:
                continue
            for q in range(power - SSTEP, power):

                def coef(y):
                    if q >= 0:
                        return coef_of(diag[own(q), pl.ds(y, 1), :])
                    return coef_of(diags[SSTEP - 1 - q if top else q + SSTEP, pl.ds(y, 1), :])

                def emit(y, value):
                    if power < SSTEP:
                        side[power, q - (power - SSTEP), y] = value
                    if q >= 0:
                        store_pieces(panel, slot(q), y, power, value)

                plane_step(
                    source(power - 1, q - 1), source(power - 1, q), source(power - 1, q + 1),
                    coef, outside if q < 0 else 1.0 / SCALE, emit,
                )
                if top and power == SSTEP and q:
                    acc = moment_sum(panel, slot(q - 1), acc)
            if top:
                acc = moment_sum(panel, power - 1, acc)
    acc = moment_sum(panel, CX - SSTEP, acc)
    mom[...] = mom_in[...] + moment_blocks(acc)


def ghost_kernel(top, info, same, following, diag, diags, side, panel, *rest):
    far_a, far_b, far_diags = rest[-3:]
    if not top:
        coef_out, count = rest[0], info[0]
        for i in range(MIDDLE - CX):
            coef_out[CX + i] = jnp.zeros((NY, NZ), F32)
        for i in range(CX):
            coef_out[SSTEP + i] = coef_of(diag[i])
        for i in range(SSTEP):
            coef_out[i] = coef_of(diags[i])
            coef_out[SSTEP + count + i] = coef_of(diags[SSTEP + i])
    if top:
        load_halo(info, same, following, None, far_a, far_diags)
    else:
        load_halo(info, same, following, far_a, None, far_diags)
    weight = jnp.where(info[2 if top else 1] > 0, 1.0 / SCALE, 0.0).astype(F32)
    buffers = (far_a, far_b)
    for power in range(SSTEP + 1):
        for q in range(power - SSTEP, 0):
            split_plane(panel, q + SSTEP, power, side.at[power], q - (power - SSTEP))
        if power == 0:
            continue
        src, dst = buffers[(power - 1) % 2], buffers[power % 2]

        def source(q):
            if q <= power - 6:
                return src, q - (power - 9)
            return side.at[power - 1], q - (power - 5)

        for q in range(power - 8, power - 4):

            def diag_row(y):
                if q >= -SSTEP:
                    return coef_of(diags[SSTEP - 1 - q if top else q + SSTEP, pl.ds(y, 1), :])
                return coef_of(far_diags[-1 - q if top else q + 2 * SSTEP, pl.ds(y, 1), :])

            def emit(y, value):
                if power < SSTEP:
                    dst[q - (power - 8), y] = value
                if q >= -SSTEP:
                    store_pieces(panel, q + SSTEP, y, power, value)

            plane_step(source(q - 1), source(q), source(q + 1), diag_row, weight, emit)


def middle_kernel(
    info, mom_in, coef, panel_in, ghost_l, ghost_u, panel, mom, iterate, field_0, field_1, field_2, field_3
):
    count = info[0]
    coefs = coef_rows(solve(mom_in[...]))

    def weight_of(plane):
        inside = (
            ((plane >= SSTEP) | (info[1] > 0))
            & ((plane < SSTEP + count) | (info[2] > 0))
            & (plane < 2 * SSTEP + count)
        )
        return jnp.where(inside, 1.0 / SCALE, 0.0).astype(F32)

    def update(store, plane, at, own):
        def emit(y, left, step):
            field_0[at, y] = left
            if own:
                iterate[at - SSTEP, y] = step

        combine(coefs, store, plane, emit)

    for i in range(MIDDLE - CX):
        field_0[CX + i] = jnp.zeros(FIELD, F32)
    for i in range(SSTEP):
        iterate[CX - SSTEP + i] = jnp.zeros(FIELD, F32)
    for p in range(SSTEP):
        update(ghost_l, p, p, False)
    for p in range(CX - SSTEP):
        update(panel_in, p, p + SSTEP, True)
    for p in range(SSTEP):
        update(panel_in, CX - SSTEP + p, count + p, True)
    for p in range(SSTEP):
        update(ghost_u, SSTEP - 1 - p, count + SSTEP + p, False)
    fields = (field_0, field_1, field_2, field_3)

    def keep_of(p):
        return (p < SSTEP + count).astype(F32)

    def apply(power, p, own):
        src = fields[power - 1]
        keep = keep_of(p)
        if own and power == 1:
            for y in range(NY):
                store_pieces(panel, p - SSTEP, y, 0, src[p, y] * keep)

        def emit(y, value):
            if power < SSTEP:
                fields[power][p, y] = value
            if own:
                store_pieces(panel, p - SSTEP, y, power, value * keep)

        plane_step(
            (src, p - 1), (src, p), (src, p + 1),
            lambda y: coef[p, pl.ds(y, 1), :], weight_of(p), emit,
        )

    def step(p, acc):
        acc = moment_sum(panel, p - 7 - SSTEP, acc)
        for power in range(SSTEP, 0, -1):
            apply(power, p - 2 * (power - 1), True)
        return acc

    def partial_step(p, acc):
        if SSTEP <= p - 7 < SSTEP + CX:
            acc = moment_sum(panel, p - 7 - SSTEP, acc)
        for power in range(SSTEP, 0, -1):
            q = p - 2 * (power - 1)
            if power <= q < MIDDLE - power:
                apply(power, q, SSTEP <= q < SSTEP + CX)
        return acc

    acc = moment_zero()
    for p in range(1, 11):
        acc = partial_step(p, acc)
    acc = lax.fori_loop(11, 20, step, acc)
    for p in range(20, 27):
        acc = partial_step(p, acc)
    mom[...] = moment_blocks(acc)


def last_kernel(info, mom_in, panel, iterate, solution_field, residual, new_field, new_residual, sems):
    rows = NY * CX
    group = 4
    coefs = coef_rows(solve(mom_in[...]))

    def copies(i):
        planes = pl.ds(i * group, group)
        return [
            pltpu.make_async_copy(new_field.at[:, planes], solution_field.at[:, planes], sems.at[0, i]),
            pltpu.make_async_copy(new_residual.at[:, planes], residual.at[:, planes], sems.at[1, i]),
        ]

    flat = NRHS * rows, NZ
    flat_field, flat_residual = new_field.reshape(flat), new_residual.reshape(flat)

    def body(i, carry):
        for k in range(group):
            p = i * group + k

            def emit(y, left, step):
                at = pl.Slice(p * NY + y, NRHS, rows)
                flat_residual[at, :] = left
                flat_field[at, :] = iterate[p, y] + step

            combine(coefs, panel, p, emit)
        for copy in copies(i):
            copy.start()
        return carry

    lax.fori_loop(0, CX // group, body, 0)
    for i in range(CX // group):
        for copy in copies(i):
            copy.wait()


SMEM_SPEC = pl.BlockSpec(memory_space=pltpu.SMEM)
VMEM_SPEC = pl.BlockSpec(memory_space=pltpu.VMEM)
HBM_SPEC = pl.BlockSpec(memory_space=pltpu.HBM)


def call(body, limit, operands, outs, scratch, kept_operands=(), far_operands=(), cost=1, aliases={}):
    operands = [
        pltpu.with_memory_space_constraint(x, pltpu.VMEM)
        if i in kept_operands
        else pltpu.with_memory_space_constraint(x, pltpu.HBM)
        if i in far_operands
        else x
        for i, x in enumerate(operands)
    ]
    return pl.pallas_call(
        body,
        out_shape=[pltpu.VMEM(s, d) if kept else jax.ShapeDtypeStruct(s, d) for s, d, kept in outs],
        in_specs=[SMEM_SPEC]
        + [HBM_SPEC if i in far_operands else VMEM_SPEC for i in range(1, len(operands))],
        out_specs=[VMEM_SPEC if kept is not None else HBM_SPEC for _, _, kept in outs],
        scratch_shapes=scratch,
        input_output_aliases=aliases,
        cost_estimate=pl.CostEstimate(
            flops=cost * 1_000_000_000, bytes_accessed=cost * 3_000_000, transcendentals=0
        ),
        compiler_params=pltpu.CompilerParams(vmem_limit_bytes=limit * 1024 * 1024),
    )(*operands)


def reduce_all(value, size, beside=()):
    if size == 128:
        rounds = ROUNDS
    else:
        rounds = [(1 << b, 2) for b in range(size.bit_length() - 1)]
    beside = list(beside)
    for order, (stride, width) in enumerate(rounds):
        total = value
        if 2 <= order < 2 + len(beside):
            total, beside[order - 2] = lax.optimization_barrier((total, beside[order - 2]))
        for turn in range(1, width):
            route = []
            for i in range(size):
                place = i // stride % width
                route.append((i, i + ((place + turn) % width - place) * stride))
            total = total + lax.ppermute(value, AXES, route)
        value = total
    return value, beside


def local(right_side, diagonal, counts):
    count = counts[0]
    size = lax.axis_size(AXES)
    me = lax.axis_index(AXES)
    info = jnp.stack([count, me, size - 1 - me]).astype(jnp.int32)

    packed = ((NRHS + 1, SSTEP, NY, NZ), F32, True)
    panel_shape = ((CX,) + PANEL, BF16, True)
    near_same, near_next, far_same, far_next = call(
        pack_kernel,
        4,
        (info, right_side, diagonal),
        [packed] * 4,
        [pltpu.SemaphoreType.DMA((8,))],
        far_operands=(1, 2),
    )
    same = [(i, i ^ 1) for i in range(size)]
    following = [(i, i + 1) for i in range(1, size - 1, 2)] + [(i + 1, i) for i in range(1, size - 1, 2)]
    halo = ((NRHS + 1) * SSTEP * NY, NZ)
    next_halo = lax.ppermute(near_next, AXES, following).reshape(halo)
    same_halo = lax.ppermute(near_same, AXES, same).reshape(halo)
    panel, mom_inner, f0, f1, f2, f3 = call(
        inner_kernel,
        8,
        (info, right_side.reshape(NRHS * CX * NY, NZ), diagonal),
        [panel_shape, ((NRHS, NZ), F32, False)] + [((CX,) + FIELD, F32, True)] * SSTEP,
        [],
        cost=4,
    )
    panel, mom, side_l, side_u, diags = call(
        edge_kernel,
        8,
        (info, same_halo, next_halo, diagonal, mom_inner, f0, f1, f2, f3, panel),
        [
            panel_shape,
            ((NRHS, NZ), F32, False),
            ((SSTEP, SSTEP) + FIELD, F32, True),
            ((SSTEP, SSTEP) + FIELD, F32, True),
            ((2 * SSTEP, NY, NZ), F32, True),
        ],
        [],
        (5, 6, 7, 8, 9),
        cost=4,
        aliases={9: 0},
    )
    mom, far_next, far_same = lax.optimization_barrier((mom, far_next, far_same))
    far_next = lax.ppermute(far_next, AXES, following).reshape(halo)
    far_same = lax.ppermute(far_same, AXES, same).reshape(halo)
    ghosts = []
    for top, side in ((False, side_l), (True, side_u)):
        ghosts.append(call(
            functools.partial(ghost_kernel, top),
            8,
            (info, far_same, far_next, diagonal, diags, side),
            [((SSTEP,) + PANEL, BF16, True)] + [((MIDDLE, NY, NZ), F32, True)] * (not top),
            [pltpu.VMEM((SSTEP,) + FIELD, F32)] * 2 + [pltpu.VMEM((2 * SSTEP, NY, NZ), F32)],
            (4, 5),
            cost=2,
        ))
    mom, ((ghost_l, coef), (ghost_u,)) = reduce_all(mom, size, ghosts)
    panel, mom, iterate = call(
        middle_kernel,
        16,
        (info, mom, coef, panel, ghost_l, ghost_u),
        [
            panel_shape,
            ((NRHS, NZ), F32, False),
            ((CX,) + FIELD, F32, True),
        ],
        [pltpu.VMEM((MIDDLE,) + FIELD, F32)] * SSTEP,
        (2, 3, 4, 5),
        cost=10,
        aliases={3: 0},
    )
    mom, _ = reduce_all(mom, size)
    shape = right_side.shape
    solution_field, residual = call(
        last_kernel,
        8,
        (info, mom, panel, iterate),
        [(shape, F32, None), (shape, F32, None)],
        [pltpu.VMEM(shape, F32), pltpu.VMEM(shape, F32), pltpu.SemaphoreType.DMA((2, CX // 4))],
        (2, 3),
        cost=4,
    )
    return (solution_field, residual)


def solution(mesh):
    in_specs = (
        P(None, AXES, None, None),
        P(AXES, None, None),
        P(AXES),
    )
    out_specs = (P(None, AXES, None, None), P(None, AXES, None, None))
    return jax.shard_map(local, mesh=mesh, in_specs=in_specs, out_specs=out_specs, check_vma=False)
```

```python
import functools

import jax
import jax.numpy as jnp
from jax import lax
from jax.experimental import pallas as pl
from jax.experimental.pallas import tpu as pltpu
from jax.sharding import PartitionSpec as P

NRHS = 16
SSTEP = 4
SHIFT = 8.5
SCALE = 7.5
CX = 16
NY = 16
NZ = 128
KB = SSTEP + 1
PIECE = KB * NRHS
ROUNDS = ((1, 2), (32, 4), (8, 4), (2, 4))
MID = CX - 2 * SSTEP
MIDDLE = CX + 2 * SSTEP
AXES = ("grp", "dom")
F32 = jnp.float32
BF16 = jnp.bfloat16
FIELD = (NY, NRHS, NZ)
PANEL = (NY, 3 * PIECE, NZ)


def over(start, stop, body, group=4):
    whole = (stop - start) // group

    def step(i, carry):
        for k in range(group):
            body(start + i * group + k)
        return carry

    if whole:
        lax.fori_loop(0, whole, step, 0)
    for plane in range(start + whole * group, stop):
        body(plane)


def pieces(value):
    hi = value.astype(BF16)
    rest = value - hi.astype(F32)
    mid = rest.astype(BF16)
    lo = (rest - mid.astype(F32)).astype(BF16)
    return hi, mid, lo


def store_pieces(panel, plane, y, power, value):
    for i, part in enumerate(pieces(value)):
        panel[plane, y, pl.ds(i * PIECE + power * NRHS, NRHS), :] = part


def split_plane(panel, at, power, field, plane):
    for y in range(NY):
        store_pieces(panel, at, y, power, field[plane, y])


def coef_of(diag):
    return (diag + (6.0 - SHIFT)) * (1.0 / SCALE)


def plane_step(below, centre_at, above, coef, weight, emit):
    lane = lax.broadcasted_iota(jnp.int32, (NRHS, NZ), 1)
    first = lane == 0
    last = lane == NZ - 1
    zero = jnp.zeros((NRHS, NZ), F32)
    src, plane = centre_at
    before = zero
    centre = src[plane, 0]
    for y in range(NY):
        after = src[plane, y + 1] if y + 1 < NY else zero
        beside = below[0][below[1], y] + above[0][above[1], y] + (before + after)
        beside = beside + jnp.where(first, 0.0, pltpu.roll(centre, 1, 1))
        beside = beside + jnp.where(last, 0.0, pltpu.roll(centre, NZ - 1, 1))
        emit(y, coef(y) * centre - weight * beside)
        before, centre = centre, after


def moment_sum(panel, plane, acc):
    for y in range(0, NY, 2):

        def rows(at, size):
            return jnp.concatenate(
                [panel[plane, y, pl.ds(at, size), :], panel[plane, y + 1, pl.ds(at, size), :]], 1
            )

        ends = [rows(at, NRHS) for at in (0, PIECE, SSTEP * NRHS, PIECE + SSTEP * NRHS)]
        acc = acc + lax.dot_general(
            rows(0, 2 * PIECE),
            jnp.concatenate(ends, 0),
            (((1,), (1,)), ((), ())),
            preferred_element_type=F32,
        )
    return acc


def moment_zero():
    return jnp.zeros((2 * PIECE, 4 * NRHS), F32)


def moment_blocks(acc):
    acc = acc[:PIECE] + acc[PIECE:]
    low = acc[:, :NRHS] + acc[:, NRHS : 2 * NRHS]
    high = acc[:, 2 * NRHS : 3 * NRHS] + acc[:, 3 * NRHS :]
    blocks = [low[j * NRHS : (j + 1) * NRHS] for j in range(KB)]
    blocks += [high[j * NRHS : (j + 1) * NRHS] for j in range(1, SSTEP)]
    return jnp.concatenate(blocks, 1)


def inverse4(m):
    def inverse2(a, b, d):
        scale = 1.0 / (a * d - b * b)
        return d * scale, -b * scale, a * scale

    p, q, r = inverse2(m[0][0], m[0][1], m[1][1])
    f00, f01 = p * m[0][2] + q * m[1][2], p * m[0][3] + q * m[1][3]
    f10, f11 = q * m[0][2] + r * m[1][2], q * m[0][3] + r * m[1][3]
    a = m[2][2] - (m[0][2] * f00 + m[1][2] * f10)
    b = m[2][3] - (m[0][2] * f01 + m[1][2] * f11)
    d = m[3][3] - (m[0][3] * f01 + m[1][3] * f11)
    u, v, w = inverse2(a, b, d)
    g00, g01 = f00 * u + f01 * v, f00 * v + f01 * w
    g10, g11 = f10 * u + f11 * v, f10 * v + f11 * w
    x00 = p + (g00 * f00 + g01 * f01)
    x01 = q + (g00 * f10 + g01 * f11)
    x11 = r + (g10 * f10 + g11 * f11)
    return [
        [x00, x01, -g00, -g01],
        [x01, x11, -g10, -g11],
        [-g00, -g10, u, v],
        [-g01, -g11, v, w],
    ]


def solve(mom):
    size = SSTEP * NRHS
    step = 4
    shifted = jnp.concatenate([mom[:, NRHS:], mom[:, :NRHS]], 1)
    band = SHIFT * mom + SCALE * shifted
    blocks = [band[:, i * NRHS : i * NRHS + size] for i in range(SSTEP)]
    work = jnp.concatenate(blocks + [mom[:, :size]], 0)
    lane = lax.broadcasted_iota(jnp.int32, (1, size), 1)
    for j in range(0, size, step):
        off = j % 8
        if off == 0 and j:
            work = work[8:]
        inside = (lane >= j) & (lane < j + step)
        rows = work[off : off + step]
        cols = [jnp.broadcast_to(rows[:, j + t : j + t + 1], (step, size)) for t in range(step)]
        inverse = inverse4([[cols[t][s : s + 1] for t in range(step)] for s in range(step)])
        new = []
        for s in range(step):
            row = inverse[s][0] * rows[0:1]
            unit = inverse[s][0]
            for t in range(1, step):
                row = row + inverse[s][t] * rows[t : t + 1]
                unit = jnp.where(lane == j + t, inverse[s][t], unit)
            new.append(jnp.where(inside, unit, row))
        acc = work[:, j : j + 1] * new[0]
        for t in range(1, step):
            acc = acc + work[:, j + t : j + t + 1] * new[t]
        work = jnp.where(inside, acc, work - acc)
    return work[8:]


def coef_rows(coef_t):
    pad = jnp.zeros((NRHS, NRHS), F32)
    eye = (
        lax.broadcasted_iota(jnp.int32, (NRHS, PIECE), 0)
        == lax.broadcasted_iota(jnp.int32, (NRHS, PIECE), 1)
    ).astype(F32)
    same = jnp.concatenate([coef_t, pad], 1)
    up = jnp.concatenate([pad, coef_t], 1)
    left = eye - (SHIFT * same + SCALE * up)
    l_hi, l_mid, l_lo = pieces(left)
    c_hi, c_mid, _ = pieces(same)
    none = jnp.zeros((NRHS, PIECE), BF16)
    rows = [
        [l_hi, l_hi, l_hi],
        [l_mid, l_mid, none],
        [l_lo, none, none],
        [c_hi, c_hi, none],
        [c_mid, none, none],
    ]
    return jnp.concatenate([jnp.concatenate(r, 1) for r in rows], 0)


def combine(coefs, panel, plane, emit):
    for y in range(0, NY, 2):
        block = jnp.concatenate([panel[plane, y], panel[plane, y + 1]], 1)
        out = jnp.dot(coefs, block, preferred_element_type=F32)
        left = out[:NRHS] + out[NRHS : 2 * NRHS] + out[2 * NRHS : 3 * NRHS]
        step = out[3 * NRHS : 4 * NRHS] + out[4 * NRHS :]
        for k in range(2):
            emit(y + k, left[:, k * NZ : (k + 1) * NZ], step[:, k * NZ : (k + 1) * NZ])


def pack(right, diag, places, sems):
    copies = []
    for i, (out, at) in enumerate(places):
        copies.append(
            pltpu.make_async_copy(
                right.at[:, pl.ds(at, SSTEP)], out.at[pl.ds(0, NRHS)], sems.at[2 * i]
            )
        )
        copies.append(
            pltpu.make_async_copy(diag.at[pl.ds(at, SSTEP)], out.at[NRHS], sems.at[2 * i + 1])
        )
    for copy in copies:
        copy.start()
    return copies


def pack_kernel(info, right, diag, near_same, near_next, far_same, far_next, sems):
    count = info[0]
    even = info[1] % 2 == 0
    places = (
        (near_same, jnp.where(even, count - SSTEP, 0)),
        (near_next, jnp.where(even, 0, count - SSTEP)),
        (far_same, jnp.where(even, count - 2 * SSTEP, SSTEP)),
        (far_next, jnp.where(even, SSTEP, count - 2 * SSTEP)),
    )
    for copy in pack(right, diag, places, sems):
        copy.wait()


def inner_kernel(info, right, diag, panel, mom, field_0, field_1, field_2, field_3):
    count = info[0]
    rows = NY * CX
    fields = (field_0, field_1, field_2, field_3)

    def load(p):
        for y in range(NY):
            field_0[p, y] = right[pl.Slice(p * NY + y, NRHS, rows), :]

    over(0, CX, load)

    def keep_of(p):
        return (p < count - SSTEP).astype(F32)

    def split(p):
        keep = keep_of(p + SSTEP)
        for y in range(NY):
            store_pieces(panel, p + SSTEP, y, 0, field_0[p + SSTEP, y] * keep)

    over(0, MID, split)
    weight = 1.0 / SCALE
    for power in range(1, SSTEP + 1):
        src = fields[power - 1]

        def apply(p, inner):
            keep = keep_of(p)

            def emit(y, value):
                if power < SSTEP:
                    fields[power][p, y] = value
                if inner:
                    store_pieces(panel, p, y, power, value * keep)

            plane_step(
                (src, p - 1), (src, p), (src, p + 1),
                lambda y: coef_of(diag[p, pl.ds(y, 1), :]), weight, emit,
            )

        for p in range(power, SSTEP):
            apply(p, False)
            apply(CX - 1 - p, False)
        over(SSTEP, CX - SSTEP, lambda p: apply(p, True))

    def two(i, acc):
        return moment_sum(panel, SSTEP + 2 * i + 1, moment_sum(panel, SSTEP + 2 * i, acc))

    mom[...] = moment_blocks(lax.fori_loop(0, MID // 2, two, moment_zero()))


def load_halo(info, same, following, field_l, field_u, diags):
    even = info[1] % 2 == 0

    def pick(at, top):
        return jnp.where(even, same[at, :], following[at, :]) if top else jnp.where(
            even, following[at, :], same[at, :]
        )

    for top, field in ((False, field_l), (True, field_u)):
        if field is None:
            continue
        for i in range(SSTEP):
            for y in range(NY):
                at = pl.Slice(i * NY + y, NRHS, SSTEP * NY)
                field[SSTEP - 1 - i if top else i, y] = pick(at, top)
            diags[i + SSTEP if top else i] = pick(pl.ds((NRHS * SSTEP + i) * NY, NY), top)


def edge_kernel(
    info, same, following, diag, mom_in, field_0, field_1, field_2, field_3, panel_in,
    panel, mom, side_l, side_u, diags,
):
    count = info[0]
    fields = (field_0, field_1, field_2, field_3)
    acc = moment_zero()
    load_halo(info, same, following, side_l.at[0], side_u.at[0], diags)
    for top in (False, True):
        side = side_u if top else side_l
        outside = jnp.where(info[2 if top else 1] > 0, 1.0 / SCALE, 0.0).astype(F32)

        def own(q):
            return count - 1 - q if top else q

        def slot(q):
            return CX - 1 - q if top else q

        for power in range(SSTEP + 1):

            def source(level, q):
                if q <= level - 1:
                    return side.at[level], q - (level - SSTEP)
                return fields[level], own(q)

            for q in range(power, SSTEP):
                split_plane(panel, slot(q), power, fields[power], own(q))
            if power == 0:
                continue
            for q in range(power - SSTEP, power):

                def coef(y):
                    if q >= 0:
                        return coef_of(diag[own(q), pl.ds(y, 1), :])
                    return coef_of(diags[SSTEP - 1 - q if top else q + SSTEP, pl.ds(y, 1), :])

                def emit(y, value):
                    if power < SSTEP:
                        side[power, q - (power - SSTEP), y] = value
                    if q >= 0:
                        store_pieces(panel, slot(q), y, power, value)

                plane_step(
                    source(power - 1, q - 1), source(power - 1, q), source(power - 1, q + 1),
                    coef, outside if q < 0 else 1.0 / SCALE, emit,
                )
                if top and power == SSTEP and q:
                    acc = moment_sum(panel, slot(q - 1), acc)
            if top:
                acc = moment_sum(panel, power - 1, acc)
    acc = moment_sum(panel, CX - SSTEP, acc)
    mom[...] = mom_in[...] + moment_blocks(acc)


def ghost_kernel(top, info, same, following, diag, diags, side, panel, *rest):
    far_a, far_b, far_diags = rest[-3:]
    if not top:
        coef_out, count = rest[0], info[0]
        for i in range(MIDDLE - CX):
            coef_out[CX + i] = jnp.zeros((NY, NZ), F32)
        for i in range(CX):
            coef_out[SSTEP + i] = coef_of(diag[i])
        for i in range(SSTEP):
            coef_out[i] = coef_of(diags[i])
            coef_out[SSTEP + count + i] = coef_of(diags[SSTEP + i])
    if top:
        load_halo(info, same, following, None, far_a, far_diags)
    else:
        load_halo(info, same, following, far_a, None, far_diags)
    weight = jnp.where(info[2 if top else 1] > 0, 1.0 / SCALE, 0.0).astype(F32)
    buffers = (far_a, far_b)
    for power in range(SSTEP + 1):
        for q in range(power - SSTEP, 0):
            split_plane(panel, q + SSTEP, power, side.at[power], q - (power - SSTEP))
        if power == 0:
            continue
        src, dst = buffers[(power - 1) % 2], buffers[power % 2]

        def source(q):
            if q <= power - 6:
                return src, q - (power - 9)
            return side.at[power - 1], q - (power - 5)

        for q in range(power - 8, power - 4):

            def diag_row(y):
                if q >= -SSTEP:
                    return coef_of(diags[SSTEP - 1 - q if top else q + SSTEP, pl.ds(y, 1), :])
                return coef_of(far_diags[-1 - q if top else q + 2 * SSTEP, pl.ds(y, 1), :])

            def emit(y, value):
                if power < SSTEP:
                    dst[q - (power - 8), y] = value
                if q >= -SSTEP:
                    store_pieces(panel, q + SSTEP, y, power, value)

            plane_step(source(q - 1), source(q), source(q + 1), diag_row, weight, emit)


def middle_kernel(
    info, mom_in, coef, panel_in, ghost_l, ghost_u, panel, mom, iterate, field_0, field_1, field_2, field_3
):
    count = info[0]
    coefs = coef_rows(solve(mom_in[...]))

    def weight_of(plane):
        inside = (
            ((plane >= SSTEP) | (info[1] > 0))
            & ((plane < SSTEP + count) | (info[2] > 0))
            & (plane < 2 * SSTEP + count)
        )
        return jnp.where(inside, 1.0 / SCALE, 0.0).astype(F32)

    def update(store, plane, at, own):
        def emit(y, left, step):
            field_0[at, y] = left
            if own:
                iterate[at - SSTEP, y] = step

        combine(coefs, store, plane, emit)

    for i in range(MIDDLE - CX):
        field_0[CX + i] = jnp.zeros(FIELD, F32)
    for i in range(SSTEP):
        iterate[CX - SSTEP + i] = jnp.zeros(FIELD, F32)
    for p in range(SSTEP):
        update(ghost_l, p, p, False)
    for p in range(CX - SSTEP):
        update(panel_in, p, p + SSTEP, True)
    for p in range(SSTEP):
        update(panel_in, CX - SSTEP + p, count + p, True)
    for p in range(SSTEP):
        update(ghost_u, SSTEP - 1 - p, count + SSTEP + p, False)
    fields = (field_0, field_1, field_2, field_3)

    def keep_of(p):
        return (p < SSTEP + count).astype(F32)

    def apply(power, p, own):
        src = fields[power - 1]
        keep = keep_of(p)
        if own and power == 1:
            for y in range(NY):
                store_pieces(panel, p - SSTEP, y, 0, src[p, y] * keep)

        def emit(y, value):
            if power < SSTEP:
                fields[power][p, y] = value
            if own:
                store_pieces(panel, p - SSTEP, y, power, value * keep)

        plane_step(
            (src, p - 1), (src, p), (src, p + 1),
            lambda y: coef[p, pl.ds(y, 1), :], weight_of(p), emit,
        )

    def step(p, acc):
        acc = moment_sum(panel, p - 7 - SSTEP, acc)
        for power in range(SSTEP, 0, -1):
            apply(power, p - 2 * (power - 1), True)
        return acc

    def partial_step(p, acc):
        if SSTEP <= p - 7 < SSTEP + CX:
            acc = moment_sum(panel, p - 7 - SSTEP, acc)
        for power in range(SSTEP, 0, -1):
            q = p - 2 * (power - 1)
            if power <= q < MIDDLE - power:
                apply(power, q, SSTEP <= q < SSTEP + CX)
        return acc

    acc = moment_zero()
    for p in range(1, 11):
        acc = partial_step(p, acc)
    acc = lax.fori_loop(11, 20, step, acc)
    for p in range(20, 27):
        acc = partial_step(p, acc)
    mom[...] = moment_blocks(acc)


def last_kernel(info, mom_in, panel, iterate, solution_field, residual, new_field, new_residual, sems):
    rows = NY * CX
    group = 4
    coefs = coef_rows(solve(mom_in[...]))

    def copies(i):
        planes = pl.ds(i * group, group)
        return [
            pltpu.make_async_copy(new_field.at[:, planes], solution_field.at[:, planes], sems.at[0, i]),
            pltpu.make_async_copy(new_residual.at[:, planes], residual.at[:, planes], sems.at[1, i]),
        ]

    flat = NRHS * rows, NZ
    flat_field, flat_residual = new_field.reshape(flat), new_residual.reshape(flat)

    def body(i, carry):
        for k in range(group):
            p = i * group + k

            def emit(y, left, step):
                at = pl.Slice(p * NY + y, NRHS, rows)
                flat_residual[at, :] = left
                flat_field[at, :] = iterate[p, y] + step

            combine(coefs, panel, p, emit)
        for copy in copies(i):
            copy.start()
        return carry

    for i in range(CX // group):
        body(i, 0)
    for i in range(CX // group):
        for copy in copies(i):
            copy.wait()


SMEM_SPEC = pl.BlockSpec(memory_space=pltpu.SMEM)
VMEM_SPEC = pl.BlockSpec(memory_space=pltpu.VMEM)
HBM_SPEC = pl.BlockSpec(memory_space=pltpu.HBM)


def call(body, limit, operands, outs, scratch, kept_operands=(), far_operands=(), cost=1, aliases={}):
    operands = [
        pltpu.with_memory_space_constraint(x, pltpu.VMEM)
        if i in kept_operands
        else pltpu.with_memory_space_constraint(x, pltpu.HBM)
        if i in far_operands
        else x
        for i, x in enumerate(operands)
    ]
    return pl.pallas_call(
        body,
        out_shape=[pltpu.VMEM(s, d) if kept else jax.ShapeDtypeStruct(s, d) for s, d, kept in outs],
        in_specs=[SMEM_SPEC]
        + [HBM_SPEC if i in far_operands else VMEM_SPEC for i in range(1, len(operands))],
        out_specs=[VMEM_SPEC if kept is not None else HBM_SPEC for _, _, kept in outs],
        scratch_shapes=scratch,
        input_output_aliases=aliases,
        cost_estimate=pl.CostEstimate(
            flops=cost * 1_000_000_000, bytes_accessed=cost * 3_000_000, transcendentals=0
        ),
        compiler_params=pltpu.CompilerParams(vmem_limit_bytes=limit * 1024 * 1024),
    )(*operands)


def reduce_all(value, size, beside=()):
    if size == 128:
        rounds = ROUNDS
    else:
        rounds = [(1 << b, 2) for b in range(size.bit_length() - 1)]
    beside = list(beside)
    for order, (stride, width) in enumerate(rounds):
        total = value
        if 2 <= order < 2 + len(beside):
            total, beside[order - 2] = lax.optimization_barrier((total, beside[order - 2]))
        for turn in range(1, width):
            route = []
            for i in range(size):
                place = i // stride % width
                route.append((i, i + ((place + turn) % width - place) * stride))
            total = total + lax.ppermute(value, AXES, route)
        value = total
    return value, beside


def local(right_side, diagonal, counts):
    count = counts[0]
    size = lax.axis_size(AXES)
    me = lax.axis_index(AXES)
    info = jnp.stack([count, me, size - 1 - me]).astype(jnp.int32)

    packed = ((NRHS + 1, SSTEP, NY, NZ), F32, True)
    panel_shape = ((CX,) + PANEL, BF16, True)
    near_same, near_next, far_same, far_next = call(
        pack_kernel,
        4,
        (info, right_side, diagonal),
        [packed] * 4,
        [pltpu.SemaphoreType.DMA((8,))],
        far_operands=(1, 2),
    )
    same = [(i, i ^ 1) for i in range(size)]
    following = [(i, i + 1) for i in range(1, size - 1, 2)] + [(i + 1, i) for i in range(1, size - 1, 2)]
    halo = ((NRHS + 1) * SSTEP * NY, NZ)
    next_halo = lax.ppermute(near_next, AXES, following).reshape(halo)
    same_halo = lax.ppermute(near_same, AXES, same).reshape(halo)
    panel, mom_inner, f0, f1, f2, f3 = call(
        inner_kernel,
        8,
        (info, right_side.reshape(NRHS * CX * NY, NZ), diagonal),
        [panel_shape, ((NRHS, NZ), F32, False)] + [((CX,) + FIELD, F32, True)] * SSTEP,
        [],
        cost=4,
    )
    panel, mom, side_l, side_u, diags = call(
        edge_kernel,
        8,
        (info, same_halo, next_halo, diagonal, mom_inner, f0, f1, f2, f3, panel),
        [
            panel_shape,
            ((NRHS, NZ), F32, False),
            ((SSTEP, SSTEP) + FIELD, F32, True),
            ((SSTEP, SSTEP) + FIELD, F32, True),
            ((2 * SSTEP, NY, NZ), F32, True),
        ],
        [],
        (5, 6, 7, 8, 9),
        cost=4,
        aliases={9: 0},
    )
    mom, far_next, far_same = lax.optimization_barrier((mom, far_next, far_same))
    far_next = lax.ppermute(far_next, AXES, following).reshape(halo)
    far_same = lax.ppermute(far_same, AXES, same).reshape(halo)
    ghosts = []
    for top, side in ((False, side_l), (True, side_u)):
        ghosts.append(call(
            functools.partial(ghost_kernel, top),
            8,
            (info, far_same, far_next, diagonal, diags, side),
            [((SSTEP,) + PANEL, BF16, True)] + [((MIDDLE, NY, NZ), F32, True)] * (not top),
            [pltpu.VMEM((SSTEP,) + FIELD, F32)] * 2 + [pltpu.VMEM((2 * SSTEP, NY, NZ), F32)],
            (4, 5),
            cost=2,
        ))
    mom, ((ghost_l, coef), (ghost_u,)) = reduce_all(mom, size, ghosts)
    panel, mom, iterate = call(
        middle_kernel,
        16,
        (info, mom, coef, panel, ghost_l, ghost_u),
        [
            panel_shape,
            ((NRHS, NZ), F32, False),
            ((CX,) + FIELD, F32, True),
        ],
        [pltpu.VMEM((MIDDLE,) + FIELD, F32)] * SSTEP,
        (2, 3, 4, 5),
        cost=10,
        aliases={3: 0},
    )
    mom, _ = reduce_all(mom, size)
    shape = right_side.shape
    solution_field, residual = call(
        last_kernel,
        8,
        (info, mom, panel, iterate),
        [(shape, F32, None), (shape, F32, None)],
        [pltpu.VMEM(shape, F32), pltpu.VMEM(shape, F32), pltpu.SemaphoreType.DMA((2, CX // 4))],
        (2, 3),
        cost=4,
    )
    return (solution_field, residual)


def solution(mesh):
    in_specs = (
        P(None, AXES, None, None),
        P(AXES, None, None),
        P(AXES),
    )
    out_specs = (P(None, AXES, None, None), P(None, AXES, None, None))
    return jax.shard_map(local, mesh=mesh, in_specs=in_specs, out_specs=out_specs, check_vma=False)
```
